256 devices in a mesh: row: 64 (over x, z, core), col: 4 (over y).
Axes of the slice: x: 4, y: 4, z: 8, core: 2. Of those that a mesh axis runs over, the one named last changes fastest.
Arguments:
- matrix: float32 [1, 64, 16, 4, 36864], P(None, 'row', None, 'col'), may hold values from -12 to 400, as said below
- panel_index: int32 [1], replicated, may hold values from 0 to 61
Outputs:
- updated: float32 [1, 64, 16, 4, 36864], P(None, 'row', None, 'col')
The draws below stay inside these ranges and needn't reach their ends.
Inputs may be any that keep to these rules, and one draw needn't show every extreme that they name: `matrix`: symmetric; each diagonal tile that the 3 steps factor is positive definite at the time it is factored.
All inputs are finite; a program needn't handle non-finite values.
Results may differ from the reference program's by a relative error of at most 0.0001.
Values sent between devices are 32-bit elements; how exact they have to be, the bound alone decides.
A program may use at most 128 MiB of HBM per device.

```python
import jax
import jax.numpy as jnp
from jax import lax

B = 192
RT = 1
ITERS = 3
TILES = 64
CT = 16
ORDER = 12288
N_ROW = 64
N_COL = 4


def draw_matrix(key, part):
    key = jax.random.fold_in(key, 11)
    first, second = jax.random.split(key, 2)
    raw = jax.random.normal(first, (ORDER, ORDER), jnp.float32)
    symmetric = (raw + raw.T) * 0.70710678
    lifted = jax.random.uniform(second, (ORDER,), jnp.float32, 66.0, 90.0)
    whole = symmetric + jnp.diag(lifted) + 0.3
    tiled = whole.reshape(RT, N_ROW, B, CT, N_COL, B).transpose(0, 1, 3, 4, 2, 5)
    return tiled.reshape(RT, N_ROW, CT, N_COL, B * B)


def setup_inputs(seed: int = 0) -> dict:
    streams_of = jax.random.split(jax.random.key(seed), 3)
    return {
        "matrix": draw_matrix(jax.random.fold_in(streams_of[2], 71), 0),
        "panel_index": jax.random.randint(streams_of[1], (1,), 0, TILES - ITERS + 1).astype(jnp.int32),
    }


def reference(matrix, panel_index):
    full = matrix.reshape(RT, N_ROW, CT, N_COL, B, B).transpose(0, 1, 4, 2, 3, 5).reshape(ORDER, ORDER)
    tile_of_row = jnp.arange(ORDER, dtype=jnp.int32) // B
    for step in range(ITERS):
        panel = panel_index[0] + step
        start = (panel * B).astype(jnp.int32)
        column = lax.dynamic_slice_in_dim(full, start, B, 1)
        block = lax.dynamic_slice_in_dim(column, start, B, 0)
        factor = jnp.linalg.cholesky(block)
        solved = lax.linalg.triangular_solve(factor, column, left_side=False, lower=True, transpose_a=True)
        below = (tile_of_row > panel)[:, None]
        lower_part = jnp.where(below, solved, jnp.zeros_like(solved))
        full = full - jnp.dot(lower_part.astype(jnp.float32), lower_part.T.astype(jnp.float32), precision=lax.Precision.HIGHEST, preferred_element_type=jnp.float32)
        placed = lax.dynamic_update_slice_in_dim(jnp.zeros_like(column), factor, start, 0)
        fresh = jnp.where(below, solved, jnp.where((tile_of_row == panel)[:, None], placed, column))
        full = lax.dynamic_update_slice_in_dim(full, fresh, start, 1)
    return full.reshape(RT, N_ROW, B, CT, N_COL, B).transpose(0, 1, 3, 4, 2, 5).reshape(matrix.shape)
```

```python
import jax
import jax.numpy as jnp
from jax import lax
from jax.experimental import pallas as pl
from jax.experimental.pallas import tpu as pltpu
from jax.sharding import PartitionSpec as P

B = 192
BLK = 32
SUB = 16
HIGH = lax.Precision.HIGHEST
F32 = jnp.float32
BF16 = jnp.bfloat16


def lanes_below(n, shape):
    return lax.broadcasted_iota(jnp.int32, shape, 1) < n


def unflatten(get, dst):
    f0, f1, f2 = get(0), get(1), get(2)
    low = lanes_below(64, f0.shape)
    zero = jnp.zeros_like(f0)
    dst[0, pl.ds(0, 96, stride=2), :] = f0
    dst[1, pl.ds(0, 96, stride=2), :] = jnp.where(low, f1, zero)
    dst[0, pl.ds(1, 96, stride=2), :] = pltpu.roll(jnp.where(low, f2, f1), 64, 1)
    dst[1, pl.ds(1, 96, stride=2), :] = jnp.where(low, pltpu.roll(f2, 64, 1), zero)


def load(ref, rows=B):
    return jnp.concatenate([ref[0, 0:rows, :], ref[1, 0:rows, :]], axis=1)


def store(ref, value):
    ref[0, 0:B, :] = value[:, :128]
    ref[1, 0:B, :] = value[:, 128:]


def flatten(even, odd):
    e0, e1 = even[:, :128], even[:, 128:]
    o0, o1 = odd[:, :128], odd[:, 128:]
    low = lanes_below(64, e0.shape)
    return e0, jnp.where(low, e1, pltpu.roll(o0, 64, 1)), pltpu.roll(jnp.where(low, o1, o0), 64, 1)


def split3(u):
    h = u.astype(BF16)
    rest = u - h.astype(F32)
    m = rest.astype(BF16)
    return h, m, (rest - m.astype(F32)).astype(BF16)


def split2(u):
    h = u.astype(BF16)
    return h, (u - h.astype(F32)).astype(BF16)


def factor_block(sa, r0):
    lo = 128 * (r0 // 128)
    hi = 384 if r0 + BLK <= 128 else 512
    width = hi - lo
    tiles = width // 128
    rows = sa[r0:r0 + BLK, lo:hi]
    diag = jnp.ones((BLK, 128), F32)
    ids = lax.broadcasted_iota(jnp.int32, (BLK, 128), 0)
    for sub in range(BLK // SUB):
        top = sub * SUB
        height = BLK - top
        live = rows[top:, :]
        col0 = r0 + top - lo
        cols = [jnp.broadcast_to(live[:, col0 + i:col0 + i + 1], (height, 128)) for i in range(SUB)]
        sub_ids = lax.broadcasted_iota(jnp.int32, (height, 128), 0)
        for j in range(SUB):
            cj = cols[j]
            pivot = cj[j:j + 1, :]
            f = jnp.where(sub_ids > j, cj * (1.0 / pivot), 0.0)
            diag = jnp.where(ids == top + j, pivot, diag)
            for i in range(j + 1, SUB):
                cols[i] = cols[i] - f * cj[i:i + 1, :]
            wide = jnp.concatenate([f] * tiles, axis=1)
            live = live - wide * live[j:j + 1, :]
        rows = live if top == 0 else jnp.concatenate([rows[:top], live], axis=0)
    u = rows * jnp.concatenate([lax.rsqrt(diag)] * tiles, axis=1)
    sa[r0:r0 + BLK, lo:hi] = u
    if r0 + BLK < B:
        h, m, l = split3(u)
        left = jnp.concatenate([h, h, m, h, m, l], axis=0)[:, :256 - lo]
        right = jnp.concatenate([h, m, h, l, m, h], axis=0)
        change = lax.dot_general(left, right, (((0,), (0,)), ((), ())), preferred_element_type=F32)
        sa[r0 + BLK:B, lo:hi] = sa[r0 + BLK:B, lo:hi] - change[r0 + BLK - lo:B - lo]


def start_tile(sa):
    r = lax.broadcasted_iota(jnp.int32, (B, 256), 0)
    c = lax.broadcasted_iota(jnp.int32, (B, 256), 1)
    sa[:, 256:512] = jnp.where(r == c, 1.0, 0.0).astype(F32)


def finish_tile(sa, linv, lfac):
    r = lax.broadcasted_iota(jnp.int32, (B, 256), 0)
    c = lax.broadcasted_iota(jnp.int32, (B, 256), 1)
    linv[0:B, :] = sa[:, 256:512]
    linv[B:256, :] = jnp.zeros((256 - B, 256), F32)
    u = jnp.where(r <= c, sa[:, 0:256], 0.0)
    full = jnp.concatenate([u, jnp.zeros((64, 256), F32)], axis=0)
    lfac[...] = full.T[0:B, :]


def nt(a, b):
    return lax.dot_general(a, b, (((1,), (1,)), ((), ())), precision=HIGH, preferred_element_type=F32)


def nn(a, b):
    return jnp.dot(a, b, precision=HIGH, preferred_element_type=F32)


def panel_step(t, g, linv, live):
    for p in range(t, 3):
        x = nt(load(g.at[t, p]), linv[t])
        if p == 2:
            x = jnp.where(live[t], x, 0.0)
        store(g.at[t, p], x)
    for s in range(t + 1, 3):
        for p in range(s - 1, 3):
            store(g.at[s, p], load(g.at[s, p]) - nt(load(g.at[t, p]), load(g.at[t, s - 1], 256)))


def weights(g, linv, w, whi, wlo):
    def full(t, p):
        return load(g.at[t, p], 256)

    w2 = nn(load(g.at[2, 2]), linv[2])
    w1 = nn(load(g.at[1, 2]) - nn(w2, full(1, 1)), linv[1])
    w0 = nn(load(g.at[0, 2]) - nn(w2, full(0, 1)) - nn(w1, full(0, 0)), linv[0])
    for t, v in enumerate((w0, w1, w2)):
        store(w.at[t], v)
    for half in range(2):
        v = jnp.concatenate([w[i // 2, i % 2, pl.ds(half, 96, stride=2), :] for i in range(6)], axis=1)
        whi[96 * half:96 * half + 96, :], wlo[96 * half:96 * half + 96, :] = split2(v)


def special_tile(special, flat, g, lfac, which, same):
    x = jnp.where(which == 0, load(g.at[0, 2]), jnp.where(which == 1, load(g.at[1, 2]), load(g.at[2, 2])))
    f = jnp.where(which == 0, lfac[0], jnp.where(which == 1, lfac[1], lfac[2]))
    store(special, jnp.where(same, f, x))
    even = jnp.concatenate([special[i, pl.ds(0, 96, stride=2), :] for i in range(2)], axis=1)
    odd = jnp.concatenate([special[i, pl.ds(1, 96, stride=2), :] for i in range(2)], axis=1)
    for i, v in enumerate(flatten(even, odd)):
        flat[pl.ds(i, 96, stride=3), :] = v


def update(c, matrix, out, panel_get, bt, whi, wlo, flat, j, panel, which, take):
    for t in range(3):
        unflatten(panel_get(c, t), bt.at[t])
    bhi, blo = split2(jnp.concatenate([bt[i // 2, i % 2] for i in range(6)], axis=1))
    dims = (((1,), (1,)), ((), ()))
    change = lax.dot_general(whi[...], bhi, dims, preferred_element_type=F32)
    change = change + lax.dot_general(wlo[...], bhi, dims, preferred_element_type=F32)
    change = change + lax.dot_general(whi[...], blo, dims, preferred_element_type=F32)
    change = jnp.concatenate([change, jnp.zeros((B, 64), F32)], axis=1)
    change = jnp.where(j > panel, change, 0.0)
    use = jnp.logical_and(take, j == panel + which)
    for i, v in enumerate(flatten(change[0:96], change[96:192])):
        old = matrix[c, pl.ds(i, 96, stride=3), :]
        out[c, pl.ds(i, 96, stride=3), :] = jnp.where(use, flat[pl.ds(i, 96, stride=3), :], old - v)


MESH = pl.DeviceIdType.MESH
N_SEM = 96


def kernel(
    panel_ref, matrix, out,
    rel, own, mask1, got1, sum1, gotz1, sum2, goty1, tile1,
    mask2, got2, sum3, gotz2, tile2, app, panels,
    sa, linv, lfac, g, w, whi, wlo, bt, special, flat,
    send_sem, recv_sem,
):
    panel = panel_ref[0]
    my_row, my_col = lax.axis_index("row"), lax.axis_index("col")
    x, z, core = my_row // 16, (my_row // 2) % 8, my_row % 2
    eight = 2 * x + core
    pair = my_row % 4
    which = lax.rem(my_col - panel + 64, 4)

    def at_y(d):
        return {"row": my_row, "col": (my_col + d) % 4}

    def at_eight(d):
        e = (eight + d) % 8
        return {"row": 16 * (e // 2) + 2 * z + e % 2, "col": my_col}

    def at_x(d):
        return {"row": (my_row + 16 * d) % 64, "col": my_col}

    def at_z(d):
        return {"row": 16 * x + 2 * ((z + d) % 8) + core, "col": my_col}

    def at_pair(u):
        return {"row": my_row - pair + u, "col": my_col}

    other_core = {"row": my_row - core + (1 - core), "col": my_col}
    count = [0]
    sent = []

    def copy(src, dst, device, start=True):
        i = count[0]
        count[0] += 1
        c = pltpu.make_async_remote_copy(
            src_ref=src, dst_ref=dst, send_sem=send_sem.at[i], recv_sem=recv_sem.at[i],
            device_id=device, device_id_type=MESH,
        )
        if start:
            c.start()
            sent.append(c)
        return c

    def arrive(copies):
        for c in copies:
            c.wait_recv()

    barrier = pltpu.get_barrier_semaphore()
    near = [at_y(d) for d in range(1, 4)] + [at_eight(d) for d in range(1, 8)] + [at_z(d) for d in range(1, 8)]
    near.append(at_pair(3 - pair))
    for device in near:
        pl.semaphore_signal(barrier, inc=1, device_id=device, device_id_type=MESH)

    slot = jnp.minimum((panel + which) // 4, 15)
    mine = matrix[slot]
    rel[0] = mine
    first = jnp.where(jnp.logical_and(my_row == panel, which == 0), mine, 0.0)
    for i in range(8):
        mask1[i] = first[36 * i:36 * i + 36]
    g[...] = jnp.zeros_like(g)
    pl.semaphore_wait(barrier, len(near))

    state = {}

    def start():
        state["first"] = [copy(mask1.at[(eight + d) % 8], got1.at[d], at_eight(d)) for d in range(1, 8)]
        state["y"] = [copy(rel.at[0], rel.at[d], at_y(d)) for d in range(1, 4)]

    def first_z():
        arrive(state["first"])
        total = mask1[eight]
        for d in range(1, 8):
            total = total + got1[d]
        sum1[...] = total
        state["first"] = [copy(sum1, gotz1.at[d], at_z(d)) for d in range(1, 8)]

    def first_y():
        arrive(state["first"])
        total = sum1[...]
        for d in range(1, 8):
            total = total + gotz1[d]
        sum2[...] = total
        state["first"] = [copy(sum2, goty1.at[d], at_y(d)) for d in range(1, 4)]

    def first_gather():
        arrive(state["first"])
        total = sum2[...]
        for d in range(1, 4):
            total = total + goty1[d]
        tile1[eight] = total
        state["first"] = [copy(tile1.at[eight], tile1.at[eight], at_eight(d)) for d in range(1, 8)]

    def first_done():
        arrive(state["first"])
        for i in range(8):
            app[0, 36 * i:36 * i + 36, :] = tile1[i]

    order = [(1, 0), (1, 1), (2, 0), (2, 1), (2, 2)]

    def row_ready():
        arrive(state["y"])
        for t in range(3):
            own[288 * t:288 * t + 288, :] = rel[(my_col - panel - t + 64) % 4]

    def rest_start():
        for n, (s, t) in enumerate(order):
            v = own[pl.ds(pl.multiple_of(288 * t + 72 * my_col, 8), 72), :]
            v = jnp.where(my_row == panel + s, v, 0.0)
            for i in range(8):
                mask2[i, n] = v[9 * i:9 * i + 9]
        state["rest"] = [copy(mask2.at[(eight + d) % 8], got2.at[d], at_eight(d)) for d in range(1, 8)]

    def rest_z():
        arrive(state["rest"])
        total = mask2[eight]
        for d in range(1, 8):
            total = total + got2[d]
        sum3[...] = total
        state["rest"] = [copy(sum3, gotz2.at[d], at_z(d)) for d in range(1, 8)]

    def rest_gather():
        arrive(state["rest"])
        total = sum3[...]
        for d in range(1, 8):
            total = total + gotz2[d]
        tile2[my_col, eight] = total
        mine = tile2.at[my_col, eight]
        state["rest"] = [copy(mine, mine, at_eight(d)) for d in range(1, 8)]

    def rest_y():
        arrive(state["rest"])
        state["rest"] = [copy(tile2.at[my_col], tile2.at[my_col], at_y(d)) for d in range(1, 4)]

    def rest_done():
        arrive(state["rest"])
        for n in range(5):
            for q in range(4):
                for i in range(8):
                    row = 72 * q + 9 * i
                    app[n + 1, row:row + 9, :] = tile2[q, i, n]

    def spread():
        base = pl.multiple_of(216 * pair, 8)
        copies = []
        for d in range(1, 4):
            u = (pair + d) % 4
            copies.append(copy(
                own.at[pl.ds(pl.multiple_of(216 * u, 8), 216)], panels.at[x, 2 * (z // 2) + u // 2, u % 2],
                at_pair(u), start=False,
            ))

        @pl.when(pair == my_col)
        def _():
            for c in copies:
                c.start()
            panels[x, z, core] = own[pl.ds(base, 216), :]

        state["spread"] = copies

    def spread_done():
        for d in range(1, 4):
            @pl.when((pair - d + 4) % 4 == my_col)
            def _():
                state["spread"][d - 1].wait_recv()

        here = panels.at[x, z, core]
        state["x"] = [copy(here, here, at_x(d)) for d in range(1, 4)]

    def ring(step):
        def block(d):
            return panels.at[:, (z + d) % 8, core]

        def half(d, h):
            return panels.at[pl.ds(2 * h, 2), (z + d) % 8, core]

        if step == 0:
            arrive(state["x"])
            state["core"] = []
        else:
            arrive(state["ring"])
        if step < 3:
            state["ring"] = [copy(block(-step), block(-step), at_z(1)), copy(block(step), block(step), at_z(-1))]
        elif step == 3:
            state["ring"] = [copy(half(-3, 0), half(-3, 0), at_z(1)), copy(half(3, 1), half(3, 1), at_z(-1))]
        for d in ([0] if step == 0 else [-step, step] if step < 4 else [4]):
            state["core"].append(copy(block(d), block(d), other_core))

    def ring_done():
        arrive(state["core"])

    def flat_rows(ref, *idx):
        return lambda o: ref[(*idx, pl.ds(o, 96, stride=3), slice(None))]

    def panel_rows(c, t):
        return lambda o: panel_rows_of(c, t, o)

    def panel_rows_of(c, t, o):
        parts, row, end = [], 288 * t, 288 * t + 288
        while row < end:
            u = row // 216
            stop = min(end, 216 * u + 216)
            parts.append(panels[c // 4, 2 * (c % 4) + u // 2, u % 2, pl.ds(row - 216 * u + o, (stop - row) // 3, stride=3), :])
            row = stop
        return jnp.concatenate(parts, axis=0)

    live = [my_row > panel + t for t in range(3)]
    comm = {
        (0, 0): [spread_done], (0, 1): [rest_z], (0, 2): [lambda: ring(0)], (0, 3): [rest_gather], (0, 4): [rest_y],
        (1, 0): [lambda: ring(1)], (1, 3): [lambda: ring(2)], (2, 0): [lambda: ring(3)], (2, 3): [lambda: ring(4)],
    }

    start()
    first_z()
    first_y()
    row_ready()
    rest_start()
    first_gather()
    spread()
    for t in range(3):
        unflatten(lambda o, t=t: own[pl.ds(288 * t + o, 96, stride=3), :], g.at[t, 2])
    first_done()
    unflatten(flat_rows(app, 0), bt.at[0])
    for t in range(3):
        sa[:, 0:256] = load(bt.at[0]) if t == 0 else load(g.at[t, t - 1])
        start_tile(sa)
        for blk in range(6):
            factor_block(sa, BLK * blk)
            for phase in comm.get((t, blk), []):
                phase()
        if t == 0:
            rest_done()
            for n, place in enumerate([(0, 0), (1, 0), (0, 1), (1, 1), (2, 1)]):
                unflatten(flat_rows(app, n + 1), g.at[place])
        finish_tile(sa, linv.at[t], lfac.at[t])
        panel_step(t, g, linv, live)
    weights(g, linv, w, whi, wlo)
    tile = panel + which
    special_tile(special, flat, g, lfac, which, my_row == tile)
    take = jnp.logical_and(which < 3, my_row >= tile)
    ring_done()

    def one(c, carry):
        update(c, matrix, out, panel_rows, bt, whi, wlo, flat, 4 * c + my_col, panel, which, take)
        return carry

    lax.fori_loop(0, 16, one, 0)
    for c in sent:
        c.wait_send()

    @pl.when(pair == my_col)
    def _():
        for c in state["spread"]:
            c.wait_send()


def body(matrix, panel_index):
    flat = matrix.reshape(16, 288, 128)
    V = pltpu.VMEM
    scratch = [
        V((4, 288, 128), F32), V((864, 128), F32), V((8, 36, 128), F32), V((8, 36, 128), F32), V((36, 128), F32),
        V((8, 36, 128), F32), V((36, 128), F32), V((4, 36, 128), F32), V((8, 36, 128), F32),
        V((8, 5, 9, 128), F32), V((8, 5, 9, 128), F32), V((5, 9, 128), F32), V((8, 5, 9, 128), F32),
        V((4, 8, 5, 9, 128), F32), V((6, 288, 128), F32), V((4, 8, 2, 216, 128), F32),
        V((B, 512), F32), V((3, 256, 256), F32), V((3, B, 256), F32), V((3, 3, 2, 256, 128), F32),
        V((3, 2, B, 128), F32), V((B, 768), BF16), V((B, 768), BF16), V((3, 2, B, 128), F32), V((2, B, 128), F32),
        V((288, 128), F32),
        pltpu.SemaphoreType.DMA((N_SEM,)), pltpu.SemaphoreType.DMA((N_SEM,)),
    ]
    out = pl.pallas_call(
        kernel,
        out_shape=jax.ShapeDtypeStruct((16, 288, 128), F32),
        in_specs=[pl.BlockSpec(memory_space=pltpu.SMEM), pl.BlockSpec(memory_space=pltpu.VMEM)],
        out_specs=pl.BlockSpec(memory_space=pltpu.VMEM),
        scratch_shapes=scratch,
        compiler_params=pltpu.CompilerParams(collective_id=0, has_side_effects=True, vmem_limit_bytes=48 << 20),
        name="panel_steps",
    )(panel_index, flat)
    return out.reshape(matrix.shape)


def solution(mesh):
    in_specs = (P(None, "row", None, "col", None), P())
    out_specs = P(None, "row", None, "col", None)
    return jax.shard_map(body, mesh=mesh, in_specs=in_specs, out_specs=out_specs, check_vma=False)
```

```python
import jax
import jax.numpy as jnp
from jax import lax
from jax.experimental import pallas as pl
from jax.experimental.pallas import tpu as pltpu
from jax.sharding import PartitionSpec as P

B = 192
BLK = 32
SUB = 16
HIGH = lax.Precision.HIGHEST
F32 = jnp.float32
BF16 = jnp.bfloat16


def lanes_below(n, shape):
    return lax.broadcasted_iota(jnp.int32, shape, 1) < n


def unflatten(get, dst):
    f0, f1, f2 = get(0), get(1), get(2)
    low = lanes_below(64, f0.shape)
    zero = jnp.zeros_like(f0)
    dst[0, pl.ds(0, 96, stride=2), :] = f0
    dst[1, pl.ds(0, 96, stride=2), :] = jnp.where(low, f1, zero)
    dst[0, pl.ds(1, 96, stride=2), :] = pltpu.roll(jnp.where(low, f2, f1), 64, 1)
    dst[1, pl.ds(1, 96, stride=2), :] = jnp.where(low, pltpu.roll(f2, 64, 1), zero)


def load(ref, rows=B):
    return jnp.concatenate([ref[0, 0:rows, :], ref[1, 0:rows, :]], axis=1)


def store(ref, value):
    ref[0, 0:B, :] = value[:, :128]
    ref[1, 0:B, :] = value[:, 128:]


def flatten(even, odd):
    e0, e1 = even[:, :128], even[:, 128:]
    o0, o1 = odd[:, :128], odd[:, 128:]
    low = lanes_below(64, e0.shape)
    return e0, jnp.where(low, e1, pltpu.roll(o0, 64, 1)), pltpu.roll(jnp.where(low, o1, o0), 64, 1)


def split3(u):
    h = u.astype(BF16)
    rest = u - h.astype(F32)
    m = rest.astype(BF16)
    return h, m, (rest - m.astype(F32)).astype(BF16)


def split2(u):
    h = u.astype(BF16)
    return h, (u - h.astype(F32)).astype(BF16)


def factor_block(sa, r0):
    lo = 128 * (r0 // 128)
    hi = 384 if r0 + BLK <= 128 else 512
    width = hi - lo
    tiles = width // 128
    rows = sa[r0:r0 + BLK, lo:hi]
    diag = jnp.ones((BLK, 128), F32)
    ids = lax.broadcasted_iota(jnp.int32, (BLK, 128), 0)
    for sub in range(BLK // SUB):
        top = sub * SUB
        height = BLK - top
        live = rows[top:, :]
        col0 = r0 + top - lo
        cols = [jnp.broadcast_to(live[:, col0 + i:col0 + i + 1], (height, 128)) for i in range(SUB)]
        sub_ids = lax.broadcasted_iota(jnp.int32, (height, 128), 0)
        for j in range(SUB):
            cj = cols[j]
            pivot = cj[j:j + 1, :]
            f = jnp.where(sub_ids > j, cj * (1.0 / pivot), 0.0)
            diag = jnp.where(ids == top + j, pivot, diag)
            for i in range(j + 1, SUB):
                cols[i] = cols[i] - f * cj[i:i + 1, :]
            wide = jnp.concatenate([f] * tiles, axis=1)
            live = live - wide * live[j:j + 1, :]
        rows = live if top == 0 else jnp.concatenate([rows[:top], live], axis=0)
    u = rows * jnp.concatenate([lax.rsqrt(diag)] * tiles, axis=1)
    sa[r0:r0 + BLK, lo:hi] = u
    if r0 + BLK < B:
        h, m, l = split3(u)
        left = jnp.concatenate([h, h, m, h, m, l], axis=0)[:, :256 - lo]
        right = jnp.concatenate([h, m, h, l, m, h], axis=0)
        change = lax.dot_general(left, right, (((0,), (0,)), ((), ())), preferred_element_type=F32)
        sa[r0 + BLK:B, lo:hi] = sa[r0 + BLK:B, lo:hi] - change[r0 + BLK - lo:B - lo]


def start_tile(sa):
    r = lax.broadcasted_iota(jnp.int32, (B, 256), 0)
    c = lax.broadcasted_iota(jnp.int32, (B, 256), 1)
    sa[:, 256:512] = jnp.where(r == c, 1.0, 0.0).astype(F32)


def finish_tile(sa, linv, lfac):
    r = lax.broadcasted_iota(jnp.int32, (B, 256), 0)
    c = lax.broadcasted_iota(jnp.int32, (B, 256), 1)
    linv[0:B, :] = sa[:, 256:512]
    linv[B:256, :] = jnp.zeros((256 - B, 256), F32)
    u = jnp.where(r <= c, sa[:, 0:256], 0.0)
    full = jnp.concatenate([u, jnp.zeros((64, 256), F32)], axis=0)
    lfac[...] = full.T[0:B, :]


def nt(a, b):
    return lax.dot_general(a, b, (((1,), (1,)), ((), ())), precision=HIGH, preferred_element_type=F32)


def nn(a, b):
    return jnp.dot(a, b, precision=HIGH, preferred_element_type=F32)


def panel_step(t, g, linv, live):
    for p in range(t, 3):
        x = nt(load(g.at[t, p]), linv[t])
        if p == 2:
            x = jnp.where(live[t], x, 0.0)
        store(g.at[t, p], x)
    for s in range(t + 1, 3):
        for p in range(s - 1, 3):
            store(g.at[s, p], load(g.at[s, p]) - nt(load(g.at[t, p]), load(g.at[t, s - 1], 256)))


def weights(g, linv, w, whi, wlo):
    def full(t, p):
        return load(g.at[t, p], 256)

    w2 = nn(load(g.at[2, 2]), linv[2])
    w1 = nn(load(g.at[1, 2]) - nn(w2, full(1, 1)), linv[1])
    w0 = nn(load(g.at[0, 2]) - nn(w2, full(0, 1)) - nn(w1, full(0, 0)), linv[0])
    for t, v in enumerate((w0, w1, w2)):
        store(w.at[t], v)
    for half in range(2):
        v = jnp.concatenate([w[i // 2, i % 2, pl.ds(half, 96, stride=2), :] for i in range(6)], axis=1)
        whi[96 * half:96 * half + 96, :], wlo[96 * half:96 * half + 96, :] = split2(v)


def special_tile(special, flat, g, lfac, which, same):
    x = jnp.where(which == 0, load(g.at[0, 2]), jnp.where(which == 1, load(g.at[1, 2]), load(g.at[2, 2])))
    f = jnp.where(which == 0, lfac[0], jnp.where(which == 1, lfac[1], lfac[2]))
    store(special, jnp.where(same, f, x))
    even = jnp.concatenate([special[i, pl.ds(0, 96, stride=2), :] for i in range(2)], axis=1)
    odd = jnp.concatenate([special[i, pl.ds(1, 96, stride=2), :] for i in range(2)], axis=1)
    for i, v in enumerate(flatten(even, odd)):
        flat[pl.ds(i, 96, stride=3), :] = v


def update(c, matrix, out, panel_get, bt, whi, wlo, flat, j, panel, which, take):
    for t in range(3):
        unflatten(panel_get(c, t), bt.at[t])
    bhi, blo = split2(jnp.concatenate([bt[i // 2, i % 2] for i in range(6)], axis=1))
    dims = (((1,), (1,)), ((), ()))
    change = lax.dot_general(whi[...], bhi, dims, preferred_element_type=F32)
    change = change + lax.dot_general(wlo[...], bhi, dims, preferred_element_type=F32)
    change = change + lax.dot_general(whi[...], blo, dims, preferred_element_type=F32)
    change = jnp.concatenate([change, jnp.zeros((B, 64), F32)], axis=1)
    change = jnp.where(j > panel, change, 0.0)
    use = jnp.logical_and(take, j == panel + which)
    for i, v in enumerate(flatten(change[0:96], change[96:192])):
        old = matrix[c, pl.ds(i, 96, stride=3), :]
        out[c, pl.ds(i, 96, stride=3), :] = jnp.where(use, flat[pl.ds(i, 96, stride=3), :], old - v)


MESH = pl.DeviceIdType.MESH
N_SEM = 256
ORDER = [(0, 0), (1, 0), (1, 1), (2, 0), (2, 1), (2, 2)]
GROUPS = [(0, 1), (1, 2), (3, 3)]
LONG, SHORT = 48, 24


def kernel(
    panel_ref, matrix, out,
    cut, got, pick, gotz0, gotz1, gotz2, tile0, tile1, tile2, rel, own, app, fresh, main, side,
    sa, linv, lfac, g, w, whi, wlo, bt, special, flat,
    send_sem, recv_sem, quarter_sem, fresh_sem,
):
    panel = panel_ref[0]
    my_row, my_col = lax.axis_index("row"), lax.axis_index("col")
    x, z, core = my_row // 16, (my_row // 2) % 8, my_row % 2
    which = lax.rem(my_col - panel + 64, 4)
    gathered = [tile0, tile1, tile2]
    gotz = [gotz0, gotz1, gotz2]

    def at(dx, dc, dy, dz=0):
        c = core if dc == 0 else 1 - core
        return {"row": 16 * ((x + dx) % 4) + 2 * ((z + dz) % 8) + c, "col": (my_col + dy) % 4}

    def at_quarter(u):
        return {"row": 16 * x + 2 * (2 * (z // 2) + u // 2) + u % 2, "col": my_row % 4}

    group = [(dx, dc, dy) for dc in range(2) for dx in range(4) for dy in range(4)][1:]
    count = [0]
    sent = []

    def copy(src, dst, device):
        i = count[0]
        count[0] += 1
        c = pltpu.make_async_remote_copy(
            src_ref=src, dst_ref=dst, send_sem=send_sem.at[i], recv_sem=recv_sem.at[i],
            device_id=device, device_id_type=MESH,
        )
        c.start()
        sent.append(c)
        return c

    def arrive(copies):
        for c in copies:
            c.wait_recv()

    barrier = pltpu.get_barrier_semaphore()
    near = [at(*d) for d in group] + [at(0, 0, 0, dz) for dz in range(1, 8)]
    across = 2 * (z // 2) + 1 - z % 2
    for dc in range(2):
        for dy in range(4):
            if dc or dy:
                near.append({"row": 16 * x + 2 * across + (core if dc == 0 else 1 - core), "col": (my_col + dy) % 4})
    for device in near:
        pl.semaphore_signal(barrier, inc=1, device_id=device, device_id_type=MESH)

    slot = jnp.minimum((panel + which) // 4, 15)
    mine = matrix[slot]
    rel[0] = mine
    for i in range(32):
        cut[i // 16, (i // 4) % 4, i % 4] = mine[9 * i:9 * i + 9]
    g[...] = jnp.zeros_like(g)
    got[x, core, my_col] = cut[core, x, my_col]
    pl.semaphore_wait(barrier, len(near))

    pieces = []
    for dx, dc, dy in group:
        c = core if dc == 0 else 1 - core
        pieces.append(copy(
            cut.at[c, (x + dx) % 4, (my_col + dy) % 4], got.at[x, core, my_col], at(dx, dc, dy),
        ))
    state = {}
    here = 2 * (z % 2) + core
    to_me = here == my_col
    quarters = []

    def send_quarters():
        for d in range(4):
            u = (here + d) % 4
            part = rel.at[0, pl.ds(pl.multiple_of(72 * u, 8), 72)]
            quarters.append(pltpu.make_async_remote_copy(
                src_ref=part, dst_ref=fresh.at[my_col], send_sem=quarter_sem.at[d], recv_sem=fresh_sem.at[my_col],
                device_id=at_quarter(u), device_id_type=MESH,
            ))
        for c in quarters[1:]:
            c.start()

        @pl.when(jnp.logical_not(to_me))
        def _():
            quarters[0].start()

        @pl.when(to_me)
        def _():
            fresh[my_col] = rel[0, pl.ds(pl.multiple_of(72 * here, 8), 72), :]

    def quarters_ready():
        for q in range(4):
            c = pltpu.make_async_remote_copy(
                src_ref=rel.at[0, pl.ds(0, 72)], dst_ref=fresh.at[q], send_sem=quarter_sem.at[0], recv_sem=fresh_sem.at[q],
                device_id=at_quarter(0), device_id_type=MESH,
            )

            @pl.when(jnp.logical_not(jnp.logical_and(to_me, my_col == q)))
            def _():
                c.wait_recv()

    def quarters_sent():
        for c in quarters[1:]:
            c.wait_send()

        @pl.when(jnp.logical_not(to_me))
        def _():
            quarters[0].wait_send()

    def pick_rows():
        arrive(pieces)
        for n, (s, t) in enumerate(ORDER):
            r = panel + s
            pick[n] = got[r // 16, r % 2, (panel + t) % 4]
        state["z"] = []
        for (a, n), dst in zip(GROUPS, gotz):
            dst[z] = pick[a:a + n]
            state["z"].append([copy(pick.at[pl.ds(a, n)], dst.at[z], at(0, 0, 0, dz)) for dz in range(1, 8)])

    def gather(i):
        arrive(state["z"][i])
        a, n = GROUPS[i]
        tile = gathered[i]
        for m in range(n):
            r = panel + ORDER[a + m][0]
            tile[core, x, my_col, m] = gotz[i][(r // 2) % 8, m]
        here = tile.at[core, x, my_col]
        members = group if i == 0 else [d for d in group if d[1] == 0]
        state[i] = [copy(here, here, at(*d)) for d in members]

    def other_core(i):
        arrive(state[i])
        half = gathered[i].at[core]
        state[i] = [copy(half, half, at(0, 1, 0))]

    def placed(i):
        arrive(state[i])
        a, n = GROUPS[i]
        for m in range(n):
            for p in range(32):
                app[a + m, 9 * p:9 * p + 9, :] = gathered[i][p // 16, (p // 4) % 4, p % 4, m]

    def row_start():
        state["y"] = [copy(rel.at[0], rel.at[d], at(0, 0, d)) for d in range(1, 4)]

    def row_ready():
        arrive(state["y"])
        for t in range(3):
            own[t] = rel[(my_col - panel - t + 64) % 4]
            unflatten(lambda o, t=t: own[t, pl.ds(o, 96, stride=3), :], g.at[t, 2])

    def bulk_start():
        for t in range(3):
            v = fresh[(panel + t) % 4]
            main[x, z, core, t] = v[:LONG]
            side[x, z, core, t] = v[LONG:]
        a, b = main.at[x, z, core], side.at[x, z, core]
        state["b"] = [copy(b, b, at(d, 0, 0)) for d in range(1, 4)]
        state["a"] = {d: copy(a, a, at(0, 0, 0, d)) for d in (1, 7, 2, 6, 3, 5, 4)}
        state["ax"] = {0: [copy(a, a, at(d, 0, 0)) for d in range(1, 4)]}
        state["core"] = []

    def a_pass(*ds):
        for d in ds:
            state["a"][d].wait_recv()
            a = main.at[x, (z - d) % 8, core]
            state["ax"][d] = [copy(a, a, at(k, 0, 0)) for k in range(1, 4)]

    def a_core(*ds):
        for d in ds:
            arrive(state["ax"][d])
            a = main.at[:, (z - d) % 8, core]
            state["core"].append(copy(a, a, at(0, 1, 0)))

    def ring(step):
        def block(d):
            return side.at[:, (z + d) % 8, core]

        def half(d, h):
            return side.at[pl.ds(2 * h, 2), (z + d) % 8, core]

        arrive(state["b"])
        if step < 3:
            state["b"] = [copy(block(-step), block(-step), at(0, 0, 0, 1)), copy(block(step), block(step), at(0, 0, 0, -1))]
        elif step == 3:
            state["b"] = [copy(half(-3, 0), half(-3, 0), at(0, 0, 0, 1)), copy(half(3, 1), half(3, 1), at(0, 0, 0, -1))]
        for d in ([0] if step == 0 else [-step, step] if step < 4 else [4]):
            state["core"].append(copy(block(d), block(d), at(0, 1, 0)))

    def panel_rows(c, t):
        def rows(o):
            parts = []
            for u in range(4):
                place = (c // 4, 2 * (c % 4) + u // 2, u % 2, t)
                parts.append(main[(*place, pl.ds(o, LONG // 3, stride=3), slice(None))])
                parts.append(side[(*place, pl.ds(o, SHORT // 3, stride=3), slice(None))])
            return jnp.concatenate(parts, axis=0)

        return rows

    def app_tile(n, place):
        unflatten(lambda o: app[n, pl.ds(o, 96, stride=3), :], place)

    live = [my_row > panel + t for t in range(3)]
    agenda = {
        (0, 1): lambda: other_core(1), (0, 2): lambda: other_core(2), (0, 3): lambda: ring(0), (0, 4): lambda: a_pass(1, 7),
        (1, 0): lambda: a_pass(2, 6), (1, 1): lambda: ring(1), (1, 2): lambda: a_pass(3, 5), (1, 3): lambda: a_pass(4),
        (1, 4): lambda: ring(2), (2, 0): lambda: a_core(0, 1, 7), (2, 1): lambda: ring(3), (2, 2): lambda: a_core(2, 6),
        (2, 4): lambda: a_core(3), (2, 5): lambda: ring(4),
    }

    send_quarters()
    pick_rows()
    for i in range(3):
        gather(i)
    quarters_ready()
    bulk_start()
    row_start()
    placed(0)
    app_tile(0, bt.at[0])
    for t in range(3):
        sa[:, 0:256] = load(bt.at[0]) if t == 0 else load(g.at[t, t - 1])
        start_tile(sa)
        for blk in range(6):
            factor_block(sa, BLK * blk)
            if (t, blk) in agenda:
                agenda[(t, blk)]()
        finish_tile(sa, linv.at[t], lfac.at[t])
        if t == 0:
            placed(1)
            placed(2)
            for n, place in enumerate([(0, 0), (1, 0), (0, 1), (1, 1), (2, 1)]):
                app_tile(n + 1, g.at[place])
            row_ready()
        panel_step(t, g, linv, live)
    weights(g, linv, w, whi, wlo)
    tile = panel + which
    special_tile(special, flat, g, lfac, which, my_row == tile)
    take = jnp.logical_and(which < 3, my_row >= tile)
    a_core(5, 4)
    arrive(state["core"])

    def one(c, carry):
        update(c, matrix, out, panel_rows, bt, whi, wlo, flat, 4 * c + my_col, panel, which, take)
        return carry

    lax.fori_loop(0, 16, one, 0)
    for c in sent:
        c.wait_send()
    quarters_sent()


def body(matrix, panel_index):
    flat = matrix.reshape(16, 288, 128)
    V = pltpu.VMEM
    scratch = [
        V((2, 4, 4, 9, 128), F32), V((4, 2, 4, 9, 128), F32), V((6, 9, 128), F32), V((8, 1, 9, 128), F32), V((8, 2, 9, 128), F32), V((8, 3, 9, 128), F32),
        V((2, 4, 4, 1, 9, 128), F32), V((2, 4, 4, 2, 9, 128), F32), V((2, 4, 4, 3, 9, 128), F32),
        V((4, 288, 128), F32), V((3, 288, 128), F32), V((6, 288, 128), F32), V((4, 72, 128), F32),
        V((4, 8, 2, 3, LONG, 128), F32), V((4, 8, 2, 3, SHORT, 128), F32),
        V((B, 512), F32), V((3, 256, 256), F32), V((3, B, 256), F32), V((3, 3, 2, 256, 128), F32),
        V((3, 2, B, 128), F32), V((B, 768), BF16), V((B, 768), BF16), V((3, 2, B, 128), F32), V((2, B, 128), F32),
        V((288, 128), F32),
        pltpu.SemaphoreType.DMA((N_SEM,)), pltpu.SemaphoreType.DMA((N_SEM,)),
        pltpu.SemaphoreType.DMA((4,)), pltpu.SemaphoreType.DMA((4,)),
    ]
    out = pl.pallas_call(
        kernel,
        out_shape=jax.ShapeDtypeStruct((16, 288, 128), F32),
        in_specs=[pl.BlockSpec(memory_space=pltpu.SMEM), pl.BlockSpec(memory_space=pltpu.VMEM)],
        out_specs=pl.BlockSpec(memory_space=pltpu.VMEM),
        scratch_shapes=scratch,
        compiler_params=pltpu.CompilerParams(collective_id=0, has_side_effects=True, vmem_limit_bytes=48 << 20),
        name="panel_steps",
    )(panel_index, flat)
    return out.reshape(matrix.shape)


def solution(mesh):
    in_specs = (P(None, "row", None, "col", None), P())
    out_specs = P(None, "row", None, "col", None)
    return jax.shard_map(body, mesh=mesh, in_specs=in_specs, out_specs=out_specs, check_vma=False)
```

```python
import jax
import jax.numpy as jnp
from jax import lax
from jax.experimental import pallas as pl
from jax.experimental.pallas import tpu as pltpu
from jax.sharding import PartitionSpec as P

B = 192
BLK = 32
SUB = 16
HIGH = lax.Precision.HIGHEST
F32 = jnp.float32
BF16 = jnp.bfloat16


def lanes_below(n, shape):
    return lax.broadcasted_iota(jnp.int32, shape, 1) < n


def unflatten(get, dst):
    f0, f1, f2 = get(0), get(1), get(2)
    low = lanes_below(64, f0.shape)
    zero = jnp.zeros_like(f0)
    dst[0, pl.ds(0, 96, stride=2), :] = f0
    dst[1, pl.ds(0, 96, stride=2), :] = jnp.where(low, f1, zero)
    dst[0, pl.ds(1, 96, stride=2), :] = pltpu.roll(jnp.where(low, f2, f1), 64, 1)
    dst[1, pl.ds(1, 96, stride=2), :] = jnp.where(low, pltpu.roll(f2, 64, 1), zero)


def load(ref, rows=B):
    return jnp.concatenate([ref[0, 0:rows, :], ref[1, 0:rows, :]], axis=1)


def store(ref, value):
    ref[0, 0:B, :] = value[:, :128]
    ref[1, 0:B, :] = value[:, 128:]


def flatten(even, odd):
    e0, e1 = even[:, :128], even[:, 128:]
    o0, o1 = odd[:, :128], odd[:, 128:]
    low = lanes_below(64, e0.shape)
    return e0, jnp.where(low, e1, pltpu.roll(o0, 64, 1)), pltpu.roll(jnp.where(low, o1, o0), 64, 1)


def split3(u):
    h = u.astype(BF16)
    rest = u - h.astype(F32)
    m = rest.astype(BF16)
    return h, m, (rest - m.astype(F32)).astype(BF16)


def split2(u):
    h = u.astype(BF16)
    return h, (u - h.astype(F32)).astype(BF16)


def factor_block(sa, r0):
    lo = 128 * (r0 // 128)
    hi = 384 if r0 + BLK <= 128 else 512
    width = hi - lo
    tiles = width // 128
    rows = sa[r0:r0 + BLK, lo:hi]
    diag = jnp.ones((BLK, 128), F32)
    ids = lax.broadcasted_iota(jnp.int32, (BLK, 128), 0)
    for sub in range(BLK // SUB):
        top = sub * SUB
        height = BLK - top
        live = rows[top:, :]
        col0 = r0 + top - lo
        cols = [jnp.broadcast_to(live[:, col0 + i:col0 + i + 1], (height, 128)) for i in range(SUB)]
        sub_ids = lax.broadcasted_iota(jnp.int32, (height, 128), 0)
        for j in range(SUB):
            cj = cols[j]
            pivot = cj[j:j + 1, :]
            f = jnp.where(sub_ids > j, cj * (1.0 / pivot), 0.0)
            diag = jnp.where(ids == top + j, pivot, diag)
            for i in range(j + 1, SUB):
                cols[i] = cols[i] - f * cj[i:i + 1, :]
            wide = jnp.concatenate([f] * tiles, axis=1)
            live = live - wide * live[j:j + 1, :]
        rows = live if top == 0 else jnp.concatenate([rows[:top], live], axis=0)
    u = rows * jnp.concatenate([lax.rsqrt(diag)] * tiles, axis=1)
    sa[r0:r0 + BLK, lo:hi] = u
    if r0 + BLK < B:
        h, m, l = split3(u)
        left = jnp.concatenate([h, h, m, h, m, l], axis=0)[:, :256 - lo]
        right = jnp.concatenate([h, m, h, l, m, h], axis=0)
        change = lax.dot_general(left, right, (((0,), (0,)), ((), ())), preferred_element_type=F32)
        sa[r0 + BLK:B, lo:hi] = sa[r0 + BLK:B, lo:hi] - change[r0 + BLK - lo:B - lo]


def start_tile(sa):
    r = lax.broadcasted_iota(jnp.int32, (B, 256), 0)
    c = lax.broadcasted_iota(jnp.int32, (B, 256), 1)
    sa[:, 256:512] = jnp.where(r == c, 1.0, 0.0).astype(F32)


def finish_tile(sa, linv, lfac):
    r = lax.broadcasted_iota(jnp.int32, (B, 256), 0)
    c = lax.broadcasted_iota(jnp.int32, (B, 256), 1)
    linv[0:B, :] = sa[:, 256:512]
    linv[B:256, :] = jnp.zeros((256 - B, 256), F32)
    u = jnp.where(r <= c, sa[:, 0:256], 0.0)
    full = jnp.concatenate([u, jnp.zeros((64, 256), F32)], axis=0)
    lfac[...] = full.T[0:B, :]


def nt(a, b):
    return lax.dot_general(a, b, (((1,), (1,)), ((), ())), precision=HIGH, preferred_element_type=F32)


def nn(a, b):
    return jnp.dot(a, b, precision=HIGH, preferred_element_type=F32)


def panel_step(t, g, linv, live):
    for p in range(t, 3):
        x = nt(load(g.at[t, p]), linv[t])
        if p == 2:
            x = jnp.where(live[t], x, 0.0)
        store(g.at[t, p], x)
    for s in range(t + 1, 3):
        for p in range(s - 1, 3):
            store(g.at[s, p], load(g.at[s, p]) - nt(load(g.at[t, p]), load(g.at[t, s - 1], 256)))


def weights(g, linv, w, whi, wlo):
    def full(t, p):
        return load(g.at[t, p], 256)

    w2 = nn(load(g.at[2, 2]), linv[2])
    w1 = nn(load(g.at[1, 2]) - nn(w2, full(1, 1)), linv[1])
    w0 = nn(load(g.at[0, 2]) - nn(w2, full(0, 1)) - nn(w1, full(0, 0)), linv[0])
    for t, v in enumerate((w0, w1, w2)):
        store(w.at[t], v)
    for half in range(2):
        v = jnp.concatenate([w[i // 2, i % 2, pl.ds(half, 96, stride=2), :] for i in range(6)], axis=1)
        whi[96 * half:96 * half + 96, :], wlo[96 * half:96 * half + 96, :] = split2(v)


def special_tile(special, flat, g, lfac, which, same):
    x = jnp.where(which == 0, load(g.at[0, 2]), jnp.where(which == 1, load(g.at[1, 2]), load(g.at[2, 2])))
    f = jnp.where(which == 0, lfac[0], jnp.where(which == 1, lfac[1], lfac[2]))
    store(special, jnp.where(same, f, x))
    even = jnp.concatenate([special[i, pl.ds(0, 96, stride=2), :] for i in range(2)], axis=1)
    odd = jnp.concatenate([special[i, pl.ds(1, 96, stride=2), :] for i in range(2)], axis=1)
    for i, v in enumerate(flatten(even, odd)):
        flat[pl.ds(i, 96, stride=3), :] = v


def convert(rows, bt, bhi, blo):
    for t in range(3):
        unflatten(rows(t), bt.at[t])
    bhi[...], blo[...] = split2(jnp.concatenate([bt[i // 2, i % 2] for i in range(6)], axis=1))


def update(c, matrix, out, bhi, blo, whi, wlo, flat, j, panel, which, take):
    dims = (((1,), (1,)), ((), ()))
    both = lax.dot_general(jnp.concatenate([whi[...], wlo[...]], axis=0), bhi[...], dims, preferred_element_type=F32)
    change = both[:B] + both[B:] + lax.dot_general(whi[...], blo[...], dims, preferred_element_type=F32)
    change = jnp.concatenate([change, jnp.zeros((B, 64), F32)], axis=1)
    change = jnp.where(j > panel, change, 0.0)
    use = jnp.logical_and(take, j == panel + which)
    for i, v in enumerate(flatten(change[0:96], change[96:192])):
        old = matrix[c, pl.ds(i, 96, stride=3), :]
        out[c, pl.ds(i, 96, stride=3), :] = jnp.where(use, flat[pl.ds(i, 96, stride=3), :], old - v)


MESH = pl.DeviceIdType.MESH
N_SEM = 256
ORDER = [(0, 0), (1, 0), (1, 1), (2, 0), (2, 1), (2, 2)]
GROUPS = [(0, 1), (1, 2), (3, 3)]
LONG, SHORT = (48, 24, 48), (24, 48, 24)
LONG_AT, SHORT_AT = (0, 48, 72), (0, 24, 72)


def kernel(
    panel_ref, source, out,
    matrix,
    cut, got, pick, gotz0, gotz1, gotz2, tile0, tile1, tile2, rel, own, app, fresh, main, side,
    sa, linv, lfac, g, w, whi, wlo, bt, bhi, blo, special, flat,
    matrix_sem, out_sem, send_sem, recv_sem, quarter_sem, fresh_sem,
):
    panel = panel_ref[0]
    my_row, my_col = lax.axis_index("row"), lax.axis_index("col")
    x, z, core = my_row // 16, (my_row // 2) % 8, my_row % 2
    which = lax.rem(my_col - panel + 64, 4)
    gathered = [tile0, tile1, tile2]
    gotz = [gotz0, gotz1, gotz2]

    def at(dx, dc, dy, dz=0):
        c = core if dc == 0 else 1 - core
        return {"row": 16 * ((x + dx) % 4) + 2 * ((z + dz) % 8) + c, "col": (my_col + dy) % 4}

    def at_quarter(u):
        return {"row": 16 * x + 2 * (2 * (z // 2) + u // 2) + u % 2, "col": my_row % 4}

    group = [(dx, dc, dy) for dc in range(2) for dx in range(4) for dy in range(4)][1:]
    count = [0]
    sent = []

    def copy(src, dst, device):
        i = count[0]
        count[0] += 1
        c = pltpu.make_async_remote_copy(
            src_ref=src, dst_ref=dst, send_sem=send_sem.at[i], recv_sem=recv_sem.at[i],
            device_id=device, device_id_type=MESH,
        )
        c.start()
        sent.append(c)
        return c

    def arrive(copies):
        for c in copies:
            c.wait_recv()

    fetch = pltpu.make_async_copy(source, matrix, matrix_sem)
    fetch.start()
    barrier = pltpu.get_barrier_semaphore()
    near = [at(*d) for d in group] + [at(0, 0, 0, dz) for dz in range(1, 8)]
    across = 2 * (z // 2) + 1 - z % 2
    for dc in range(2):
        for dy in range(4):
            if dc or dy:
                near.append({"row": 16 * x + 2 * across + (core if dc == 0 else 1 - core), "col": (my_col + dy) % 4})
    for device in near:
        pl.semaphore_signal(barrier, inc=1, device_id=device, device_id_type=MESH)

    g[...] = jnp.zeros_like(g)
    slot = jnp.minimum((panel + which) // 4, 15)
    fetch.wait()
    mine = matrix[slot]
    rel[0] = mine
    for i in range(32):
        cut[i // 16, (i // 4) % 4, i % 4] = mine[9 * i:9 * i + 9]
    got[x, core, my_col] = cut[core, x, my_col]
    pl.semaphore_wait(barrier, len(near))

    pieces = []
    for dx, dc, dy in group:
        c = core if dc == 0 else 1 - core
        pieces.append(copy(
            cut.at[c, (x + dx) % 4, (my_col + dy) % 4], got.at[x, core, my_col], at(dx, dc, dy),
        ))
    state = {}
    here = 2 * (z % 2) + core
    to_me = here == my_col
    quarters = []

    def send_quarters():
        for d in range(4):
            u = (here + d) % 4
            part = rel.at[0, pl.ds(pl.multiple_of(72 * u, 8), 72)]
            quarters.append(pltpu.make_async_remote_copy(
                src_ref=part, dst_ref=fresh.at[my_col], send_sem=quarter_sem.at[d], recv_sem=fresh_sem.at[my_col],
                device_id=at_quarter(u), device_id_type=MESH,
            ))
        for c in quarters[1:]:
            c.start()

        @pl.when(jnp.logical_not(to_me))
        def _():
            quarters[0].start()

        @pl.when(to_me)
        def _():
            fresh[my_col] = rel[0, pl.ds(pl.multiple_of(72 * here, 8), 72), :]

    def quarters_ready():
        for q in range(4):
            c = pltpu.make_async_remote_copy(
                src_ref=rel.at[0, pl.ds(0, 72)], dst_ref=fresh.at[q], send_sem=quarter_sem.at[0], recv_sem=fresh_sem.at[q],
                device_id=at_quarter(0), device_id_type=MESH,
            )

            @pl.when(jnp.logical_not(jnp.logical_and(to_me, my_col == q)))
            def _():
                c.wait_recv()

    def quarters_sent():
        for c in quarters[1:]:
            c.wait_send()

        @pl.when(jnp.logical_not(to_me))
        def _():
            quarters[0].wait_send()

    def pick_rows():
        arrive(pieces)
        for n, (s, t) in enumerate(ORDER):
            r = panel + s
            pick[n] = got[r // 16, r % 2, (panel + t) % 4]
        state["z"] = []
        for (a, n), dst in zip(GROUPS, gotz):
            dst[z] = pick[a:a + n]
            state["z"].append([copy(pick.at[pl.ds(a, n)], dst.at[z], at(0, 0, 0, dz)) for dz in range(1, 8)])

    def gather(i):
        arrive(state["z"][i])
        a, n = GROUPS[i]
        tile = gathered[i]
        for m in range(n):
            r = panel + ORDER[a + m][0]
            tile[core, x, my_col, m] = gotz[i][(r // 2) % 8, m]
        here = tile.at[core, x, my_col]
        members = group if i == 0 else [d for d in group if d[1] == 0]
        state[i] = [copy(here, here, at(*d)) for d in members]

    def other_core(i):
        arrive(state[i])
        half = gathered[i].at[core]
        state[i] = [copy(half, half, at(0, 1, 0))]

    def placed(i):
        arrive(state[i])
        a, n = GROUPS[i]
        for m in range(n):
            for p in range(32):
                app[a + m, 9 * p:9 * p + 9, :] = gathered[i][p // 16, (p // 4) % 4, p % 4, m]

    def row_start():
        state["y"] = [copy(rel.at[0], rel.at[d], at(0, 0, d)) for d in range(1, 4)]

    def row_ready():
        arrive(state["y"])
        for t in range(3):
            own[t] = rel[(my_col - panel - t + 64) % 4]
            unflatten(lambda o, t=t: own[t, pl.ds(o, 96, stride=3), :], g.at[t, 2])

    def main_block(d):
        return main.at[x, (z + d) % 8, core]

    def pass_x(d):
        state["ax"][d] = [copy(main_block(d), main_block(d), at(k, 0, 0)) for k in range(1, 4)]

    def bulk_start():
        for t in range(3):
            v = fresh[(panel + t) % 4]
            main[x, z, core, LONG_AT[t]:LONG_AT[t] + LONG[t], :] = v[:LONG[t]]
            side[x, z, core, SHORT_AT[t]:SHORT_AT[t] + SHORT[t], :] = v[LONG[t]:]
        state["core"], state["ax"] = [], {}
        main_ring(0)
        b = side.at[x, z, core]
        state["b"] = [copy(b, b, at(d, 0, 0)) for d in range(1, 4)]

    def main_ring(step):
        def part(d, h):
            return main.at[x, (z + d) % 8, core, pl.ds(64 * h, 64 - 8 * h)]

        if step > 0:
            arrive(state["a"])
        if step < 3:
            state["a"] = [
                copy(main_block(-step), main_block(-step), at(0, 0, 0, 1)),
                copy(main_block(step), main_block(step), at(0, 0, 0, -1)),
            ]
        elif step == 3:
            state["a"] = [
                copy(part(-3, 0), part(-3, 0), at(0, 0, 0, 1)), copy(part(3, 1), part(3, 1), at(0, 0, 0, -1)),
            ]
        for d in ([0] if step == 0 else [-step, step] if step < 4 else [4]):
            pass_x(d)

    def main_core(*ds):
        for d in ds:
            arrive(state["ax"][d])
            a = main.at[:, (z + d) % 8, core]
            state["core"].append(copy(a, a, at(0, 1, 0)))

    def side_ring(step):
        def block(d):
            return side.at[:, (z + d) % 8, core]

        def half(d, h):
            return side.at[pl.ds(2 * h, 2), (z + d) % 8, core]

        arrive(state["b"])
        if step < 3:
            state["b"] = [copy(block(-step), block(-step), at(0, 0, 0, 1)), copy(block(step), block(step), at(0, 0, 0, -1))]
        elif step == 3:
            state["b"] = [copy(half(-3, 0), half(-3, 0), at(0, 0, 0, 1)), copy(half(3, 1), half(3, 1), at(0, 0, 0, -1))]
        for d in ([0] if step == 0 else [-step, step] if step < 4 else [4]):
            state["core"].append(copy(block(d), block(d), at(0, 1, 0)))

    def panel_rows(c, t):
        def rows(o):
            parts = []
            for u in range(4):
                place = (c // 4, 2 * (c % 4) + u // 2, u % 2)
                parts.append(main[(*place, pl.ds(LONG_AT[t] + o, LONG[t] // 3, stride=3), slice(None))])
                parts.append(side[(*place, pl.ds(SHORT_AT[t] + o, SHORT[t] // 3, stride=3), slice(None))])
            return jnp.concatenate(parts, axis=0)

        return rows

    def app_tile(n, place):
        unflatten(lambda o: app[n, pl.ds(o, 96, stride=3), :], place)

    live = [my_row > panel + t for t in range(3)]
    agenda = {
        (0, 0): lambda: other_core(1), (0, 1): lambda: other_core(2), (0, 2): lambda: main_ring(2),
        (0, 4): lambda: side_ring(1), (1, 0): lambda: main_ring(3), (1, 2): lambda: side_ring(2),
        (1, 3): lambda: main_ring(4), (1, 5): lambda: main_core(0, -1, 1), (2, 0): lambda: side_ring(3),
        (2, 2): lambda: main_core(-2, 2), (2, 4): lambda: side_ring(4), (2, 5): lambda: main_core(-3, 3),
    }

    send_quarters()
    pick_rows()
    quarters_ready()
    bulk_start()
    for i in range(3):
        gather(i)
    row_start()
    main_ring(1)
    side_ring(0)
    placed(0)
    app_tile(0, bt.at[0, 0])
    for t in range(3):
        sa[:, 0:256] = load(bt.at[0, 0]) if t == 0 else load(g.at[t, t - 1])
        start_tile(sa)
        for blk in range(6):
            factor_block(sa, BLK * blk)
            if (t, blk) in agenda:
                agenda[(t, blk)]()
        finish_tile(sa, linv.at[t], lfac.at[t])
        if t == 0:
            placed(1)
            placed(2)
            for n, place in enumerate([(0, 0), (1, 0), (0, 1), (1, 1), (2, 1)]):
                app_tile(n + 1, g.at[place])
            row_ready()
        panel_step(t, g, linv, live)
    weights(g, linv, w, whi, wlo)
    tile = panel + which
    special_tile(special, flat, g, lfac, which, my_row == tile)
    take = jnp.logical_and(which < 3, my_row >= tile)
    main_core(4)
    arrive(state["core"])

    def one(c, carry):
        for i in range(4):
            convert(lambda t, i=i: panel_rows(4 * c + i, t), bt.at[i], bhi.at[i], blo.at[i])
        for i in range(4):
            j = 4 * (4 * c + i) + my_col
            update(4 * c + i, matrix, matrix, bhi.at[i], blo.at[i], whi, wlo, flat, j, panel, which, take)
        back(c).start()
        return carry

    def back(c):
        return pltpu.make_async_copy(matrix.at[pl.ds(4 * c, 4)], out.at[pl.ds(4 * c, 4)], out_sem.at[c])

    lax.fori_loop(0, 4, one, 0)
    for c in range(4):
        back(c).wait()
    for c in sent:
        c.wait_send()
    quarters_sent()


def body(matrix, panel_index):
    flat = matrix.reshape(16, 288, 128)
    V = pltpu.VMEM
    scratch = [
        V((16, 288, 128), F32),
        V((2, 4, 4, 9, 128), F32), V((4, 2, 4, 9, 128), F32), V((6, 9, 128), F32), V((8, 1, 9, 128), F32), V((8, 2, 9, 128), F32), V((8, 3, 9, 128), F32),
        V((2, 4, 4, 1, 9, 128), F32), V((2, 4, 4, 2, 9, 128), F32), V((2, 4, 4, 3, 9, 128), F32),
        V((4, 288, 128), F32), V((3, 288, 128), F32), V((6, 288, 128), F32), V((4, 72, 128), F32),
        V((4, 8, 2, sum(LONG), 128), F32), V((4, 8, 2, sum(SHORT), 128), F32),
        V((B, 512), F32), V((3, 256, 256), F32), V((3, B, 256), F32), V((3, 3, 2, 256, 128), F32),
        V((3, 2, B, 128), F32), V((B, 768), BF16), V((B, 768), BF16), V((4, 3, 2, B, 128), F32),
        V((4, B, 768), BF16), V((4, B, 768), BF16), V((2, B, 128), F32), V((288, 128), F32), pltpu.SemaphoreType.DMA,
        pltpu.SemaphoreType.DMA((4,)),
        pltpu.SemaphoreType.DMA((N_SEM,)), pltpu.SemaphoreType.DMA((N_SEM,)),
        pltpu.SemaphoreType.DMA((4,)), pltpu.SemaphoreType.DMA((4,)),
    ]
    out = pl.pallas_call(
        kernel,
        out_shape=jax.ShapeDtypeStruct((16, 288, 128), F32),
        in_specs=[pl.BlockSpec(memory_space=pltpu.SMEM), pl.BlockSpec(memory_space=pltpu.HBM)],
        out_specs=pl.BlockSpec(memory_space=pltpu.HBM),
        scratch_shapes=scratch,
        compiler_params=pltpu.CompilerParams(collective_id=0, has_side_effects=True, vmem_limit_bytes=60 << 20),
        name="panel_steps",
    )(panel_index, flat)
    return out.reshape(matrix.shape)


def solution(mesh):
    in_specs = (P(None, "row", None, "col", None), P())
    out_specs = P(None, "row", None, "col", None)
    return jax.shard_map(body, mesh=mesh, in_specs=in_specs, out_specs=out_specs, check_vma=False)
```

```python
import jax
import jax.numpy as jnp
from jax import lax
from jax.experimental import pallas as pl
from jax.experimental.pallas import tpu as pltpu
from jax.sharding import PartitionSpec as P

B = 192
BLK = 32
SUB = 16
HIGH = lax.Precision.HIGHEST
F32 = jnp.float32
BF16 = jnp.bfloat16


def lanes_below(n, shape):
    return lax.broadcasted_iota(jnp.int32, shape, 1) < n


def unflatten(get, dst):
    f0, f1, f2 = get(0), get(1), get(2)
    low = lanes_below(64, f0.shape)
    zero = jnp.zeros_like(f0)
    dst[0, pl.ds(0, 96, stride=2), :] = f0
    dst[1, pl.ds(0, 96, stride=2), :] = jnp.where(low, f1, zero)
    dst[0, pl.ds(1, 96, stride=2), :] = pltpu.roll(jnp.where(low, f2, f1), 64, 1)
    dst[1, pl.ds(1, 96, stride=2), :] = jnp.where(low, pltpu.roll(f2, 64, 1), zero)


def load(ref, rows=B):
    return jnp.concatenate([ref[0, 0:rows, :], ref[1, 0:rows, :]], axis=1)


def store(ref, value):
    ref[0, 0:B, :] = value[:, :128]
    ref[1, 0:B, :] = value[:, 128:]


def flatten(even, odd):
    e0, e1 = even[:, :128], even[:, 128:]
    o0, o1 = odd[:, :128], odd[:, 128:]
    low = lanes_below(64, e0.shape)
    return e0, jnp.where(low, e1, pltpu.roll(o0, 64, 1)), pltpu.roll(jnp.where(low, o1, o0), 64, 1)


def split3(u):
    h = u.astype(BF16)
    rest = u - h.astype(F32)
    m = rest.astype(BF16)
    return h, m, (rest - m.astype(F32)).astype(BF16)


def split2(u):
    h = u.astype(BF16)
    return h, (u - h.astype(F32)).astype(BF16)


def factor_block(sa, r0):
    lo = 128 * (r0 // 128)
    hi = 384 if r0 + BLK <= 128 else 512
    width = hi - lo
    tiles = width // 128
    rows = sa[r0:r0 + BLK, lo:hi]
    diag = jnp.ones((BLK, 128), F32)
    ids = lax.broadcasted_iota(jnp.int32, (BLK, 128), 0)
    for sub in range(BLK // SUB):
        top = sub * SUB
        height = BLK - top
        live = rows[top:, :]
        col0 = r0 + top - lo
        cols = [jnp.broadcast_to(live[:, col0 + i:col0 + i + 1], (height, 128)) for i in range(SUB)]
        sub_ids = lax.broadcasted_iota(jnp.int32, (height, 128), 0)
        for j in range(SUB):
            cj = cols[j]
            pivot = cj[j:j + 1, :]
            f = jnp.where(sub_ids > j, cj * (1.0 / pivot), 0.0)
            diag = jnp.where(ids == top + j, pivot, diag)
            for i in range(j + 1, SUB):
                cols[i] = cols[i] - f * cj[i:i + 1, :]
            wide = jnp.concatenate([f] * tiles, axis=1)
            live = live - wide * live[j:j + 1, :]
        rows = live if top == 0 else jnp.concatenate([rows[:top], live], axis=0)
    u = rows * jnp.concatenate([lax.rsqrt(diag)] * tiles, axis=1)
    sa[r0:r0 + BLK, lo:hi] = u
    if r0 + BLK < B:
        h, m, l = split3(u)
        left = jnp.concatenate([h, h, m, h, m, l], axis=0)[:, :256 - lo]
        right = jnp.concatenate([h, m, h, l, m, h], axis=0)
        change = lax.dot_general(left, right, (((0,), (0,)), ((), ())), preferred_element_type=F32)
        sa[r0 + BLK:B, lo:hi] = sa[r0 + BLK:B, lo:hi] - change[r0 + BLK - lo:B - lo]


def start_tile(sa):
    r = lax.broadcasted_iota(jnp.int32, (B, 256), 0)
    c = lax.broadcasted_iota(jnp.int32, (B, 256), 1)
    sa[:, 256:512] = jnp.where(r == c, 1.0, 0.0).astype(F32)


def finish_tile(sa, linv, lfac):
    r = lax.broadcasted_iota(jnp.int32, (B, 256), 0)
    c = lax.broadcasted_iota(jnp.int32, (B, 256), 1)
    linv[0:B, :] = sa[:, 256:512]
    linv[B:256, :] = jnp.zeros((256 - B, 256), F32)
    u = jnp.where(r <= c, sa[:, 0:256], 0.0)
    full = jnp.concatenate([u, jnp.zeros((64, 256), F32)], axis=0)
    lfac[...] = full.T[0:B, :]


def nt(a, b):
    return lax.dot_general(a, b, (((1,), (1,)), ((), ())), precision=HIGH, preferred_element_type=F32)


def nn(a, b):
    return jnp.dot(a, b, precision=HIGH, preferred_element_type=F32)


def panel_step(t, g, linv):
    for p in range(t, 2):
        store(g.at[t, p], nt(load(g.at[t, p]), linv[t]))
    for s in range(t + 1, 3):
        for p in range(s - 1, 2):
            store(g.at[s, p], load(g.at[s, p]) - nt(load(g.at[t, p]), load(g.at[t, s - 1], 256)))


def own_step(t, g, linv, live):
    v = jnp.where(live[t], nt(load(g.at[t, 2]), linv[t]), 0.0)
    store(g.at[t, 2], v)
    for s in range(t + 1, 3):
        store(g.at[s, 2], load(g.at[s, 2]) - nt(v, load(g.at[t, s - 1], 256)))


def weights(g, linv, w, whi, wlo):
    def full(t, p):
        return load(g.at[t, p], 256)

    w2 = nn(load(g.at[2, 2]), linv[2])
    w1 = nn(load(g.at[1, 2]) - nn(w2, full(1, 1)), linv[1])
    w0 = nn(load(g.at[0, 2]) - nn(w2, full(0, 1)) - nn(w1, full(0, 0)), linv[0])
    for t, v in enumerate((w0, w1, w2)):
        store(w.at[t], v)
    for half in range(2):
        v = jnp.concatenate([w[i // 2, i % 2, pl.ds(half, 96, stride=2), :] for i in range(6)], axis=1)
        whi[96 * half:96 * half + 96, :], wlo[96 * half:96 * half + 96, :] = split2(v)


def special_tile(special, flat, g, lfac, which, same):
    x = jnp.where(which == 0, load(g.at[0, 2]), jnp.where(which == 1, load(g.at[1, 2]), load(g.at[2, 2])))
    f = jnp.where(which == 0, lfac[0], jnp.where(which == 1, lfac[1], lfac[2]))
    store(special, jnp.where(same, f, x))
    even = jnp.concatenate([special[i, pl.ds(0, 96, stride=2), :] for i in range(2)], axis=1)
    odd = jnp.concatenate([special[i, pl.ds(1, 96, stride=2), :] for i in range(2)], axis=1)
    for i, v in enumerate(flatten(even, odd)):
        flat[pl.ds(i, 96, stride=3), :] = v


def convert(rows, bt, bhi, blo):
    for t in range(3):
        unflatten(rows(t), bt.at[t])
    bhi[...], blo[...] = split2(jnp.concatenate([bt[i // 2, i % 2] for i in range(6)], axis=1))


def update(c, matrix, out, bhi, blo, whi, wlo, flat, j, panel, which, take):
    dims = (((1,), (1,)), ((), ()))
    both = lax.dot_general(jnp.concatenate([whi[...], wlo[...]], axis=0), bhi[...], dims, preferred_element_type=F32)
    change = both[:B] + both[B:] + lax.dot_general(whi[...], blo[...], dims, preferred_element_type=F32)
    change = jnp.concatenate([change, jnp.zeros((B, 64), F32)], axis=1)
    change = jnp.where(j > panel, change, 0.0)
    use = jnp.logical_and(take, j == panel + which)
    for i, v in enumerate(flatten(change[0:96], change[96:192])):
        old = matrix[c, pl.ds(i, 96, stride=3), :]
        out[c, pl.ds(i, 96, stride=3), :] = jnp.where(use, flat[pl.ds(i, 96, stride=3), :], old - v)


MESH = pl.DeviceIdType.MESH
N_SEM = 256
ORDER = [(0, 0), (1, 0), (1, 1), (2, 0), (2, 1), (2, 2)]
GROUPS = [(0, 1), (1, 2), (3, 3)]
LONG, SHORT = (48, 24, 48), (24, 48, 24)
LONG_AT, SHORT_AT = (0, 48, 72), (0, 24, 72)


def kernel(
    panel_ref, matrix, out,
    cut, got, pick, gotz0, gotz1, gotz2, tile0, tile1, tile2, rel, own, app, fresh, main, side,
    sa, linv, lfac, g, w, whi, wlo, bt, bhi, blo, special, flat,
    send_sem, recv_sem, quarter_sem, fresh_sem,
):
    panel = panel_ref[0]
    my_row, my_col = lax.axis_index("row"), lax.axis_index("col")
    x, z, core = my_row // 16, (my_row // 2) % 8, my_row % 2
    which = lax.rem(my_col - panel + 64, 4)
    gathered = [tile0, tile1, tile2]
    gotz = [gotz0, gotz1, gotz2]

    def at(dx, dc, dy, dz=0):
        c = core if dc == 0 else 1 - core
        return {"row": 16 * ((x + dx) % 4) + 2 * ((z + dz) % 8) + c, "col": (my_col + dy) % 4}

    def at_quarter(u):
        return {"row": 16 * x + 2 * (2 * (z // 2) + u // 2) + u % 2, "col": my_row % 4}

    group = [(dx, dc, dy) for dc in range(2) for dx in range(4) for dy in range(4)][1:]
    count = [0]
    sent = []

    def copy(src, dst, device):
        i = count[0]
        count[0] += 1
        c = pltpu.make_async_remote_copy(
            src_ref=src, dst_ref=dst, send_sem=send_sem.at[i], recv_sem=recv_sem.at[i],
            device_id=device, device_id_type=MESH,
        )
        c.start()
        sent.append(c)
        return c

    def arrive(copies):
        for c in copies:
            c.wait_recv()

    barrier = pltpu.get_barrier_semaphore()
    near = [at(*d) for d in group] + [at(0, 0, 0, dz) for dz in range(1, 8)]
    across = 2 * (z // 2) + 1 - z % 2
    for dc in range(2):
        for dy in range(4):
            if dc or dy:
                near.append({"row": 16 * x + 2 * across + (core if dc == 0 else 1 - core), "col": (my_col + dy) % 4})
    for device in near:
        pl.semaphore_signal(barrier, inc=1, device_id=device, device_id_type=MESH)

    g[...] = jnp.zeros_like(g)
    slot = jnp.minimum((panel + which) // 4, 15)
    mine = matrix[slot]
    rel[0] = mine
    for i in range(32):
        cut[i // 16, (i // 4) % 4, i % 4] = mine[9 * i:9 * i + 9]
    got[x, core, my_col] = cut[core, x, my_col]
    pl.semaphore_wait(barrier, len(near))

    pieces = []
    for dx, dc, dy in group:
        c = core if dc == 0 else 1 - core
        pieces.append(copy(
            cut.at[c, (x + dx) % 4, (my_col + dy) % 4], got.at[x, core, my_col], at(dx, dc, dy),
        ))
    state = {}
    here = 2 * (z % 2) + core
    to_me = here == my_col
    quarters = []

    def send_quarters():
        for d in range(4):
            u = (here + d) % 4
            part = rel.at[0, pl.ds(pl.multiple_of(72 * u, 8), 72)]
            quarters.append(pltpu.make_async_remote_copy(
                src_ref=part, dst_ref=fresh.at[my_col], send_sem=quarter_sem.at[d], recv_sem=fresh_sem.at[my_col],
                device_id=at_quarter(u), device_id_type=MESH,
            ))
        for c in quarters[1:]:
            c.start()

        @pl.when(jnp.logical_not(to_me))
        def _():
            quarters[0].start()

        @pl.when(to_me)
        def _():
            fresh[my_col] = rel[0, pl.ds(pl.multiple_of(72 * here, 8), 72), :]

    def quarters_ready():
        for q in range(4):
            c = pltpu.make_async_remote_copy(
                src_ref=rel.at[0, pl.ds(0, 72)], dst_ref=fresh.at[q], send_sem=quarter_sem.at[0], recv_sem=fresh_sem.at[q],
                device_id=at_quarter(0), device_id_type=MESH,
            )

            @pl.when(jnp.logical_not(jnp.logical_and(to_me, my_col == q)))
            def _():
                c.wait_recv()

    def quarters_sent():
        for c in quarters[1:]:
            c.wait_send()

        @pl.when(jnp.logical_not(to_me))
        def _():
            quarters[0].wait_send()

    def pick_rows():
        arrive(pieces)
        for n, (s, t) in enumerate(ORDER):
            r = panel + s
            pick[n] = got[r // 16, r % 2, (panel + t) % 4]
        state["z"] = []
        for (a, n), dst in zip(GROUPS, gotz):
            dst[z] = pick[a:a + n]
            state["z"].append([copy(pick.at[pl.ds(a, n)], dst.at[z], at(0, 0, 0, dz)) for dz in range(1, 8)])

    def gather(i):
        arrive(state["z"][i])
        a, n = GROUPS[i]
        tile = gathered[i]
        for m in range(n):
            r = panel + ORDER[a + m][0]
            tile[core, x, my_col, m] = gotz[i][(r // 2) % 8, m]
        here = tile.at[core, x, my_col]
        members = group if i == 0 else [d for d in group if d[1] == 0]
        state[i] = [copy(here, here, at(*d)) for d in members]

    def other_core(i):
        arrive(state[i])
        half = gathered[i].at[core]
        state[i] = [copy(half, half, at(0, 1, 0))]

    def placed(i):
        arrive(state[i])
        a, n = GROUPS[i]
        for m in range(n):
            for p in range(32):
                app[a + m, 9 * p:9 * p + 9, :] = gathered[i][p // 16, (p // 4) % 4, p % 4, m]

    def row_start():
        state["y"] = [copy(rel.at[0], rel.at[d], at(0, 0, d)) for d in range(1, 4)]

    def row_ready():
        arrive(state["y"])
        for t in range(3):
            own[t] = rel[(my_col - panel - t + 64) % 4]
            unflatten(lambda o, t=t: own[t, pl.ds(o, 96, stride=3), :], g.at[t, 2])

    def main_block(d):
        return main.at[x, (z + d) % 8, core]

    def pass_x(d):
        state["ax"][d] = [copy(main_block(d), main_block(d), at(k, 0, 0)) for k in range(1, 4)]

    def bulk_start():
        for t in range(3):
            v = fresh[(panel + t) % 4]
            main[x, z, core, LONG_AT[t]:LONG_AT[t] + LONG[t], :] = v[:LONG[t]]
            side[x, z, core, SHORT_AT[t]:SHORT_AT[t] + SHORT[t], :] = v[LONG[t]:]
        state["core"], state["ax"] = [], {}
        main_ring(0)
        b = side.at[x, z, core]
        state["b"] = {}
        state["bx"] = {d: copy(b, b, at(d, 0, 0)) for d in range(1, 4)}
        side_ring(0, 0)

    def main_ring(step):
        def part(d, h):
            return main.at[x, (z + d) % 8, core, pl.ds(64 * h, 64 - 8 * h)]

        if step > 0:
            arrive(state["a"])
        if step < 3:
            state["a"] = [
                copy(main_block(-step), main_block(-step), at(0, 0, 0, 1)),
                copy(main_block(step), main_block(step), at(0, 0, 0, -1)),
            ]
        elif step == 3:
            state["a"] = [
                copy(part(-3, 0), part(-3, 0), at(0, 0, 0, 1)), copy(part(3, 1), part(3, 1), at(0, 0, 0, -1)),
            ]
        for d in ([0] if step == 0 else [-step, step] if step < 4 else [4]):
            pass_x(d)

    def main_core(*ds):
        for d in ds:
            arrive(state["ax"][d])
            a = main.at[:, (z + d) % 8, core]
            state["core"].append(copy(a, a, at(0, 1, 0)))

    def side_ring(step, *ks):
        def block(k, d):
            return side.at[(x + k) % 4, (z + d) % 8, core]

        def half(k, d, h):
            return side.at[(x + k) % 4, (z + d) % 8, core, pl.ds(48 * h, 48)]

        for k in ks:
            if step > 0:
                arrive(state["b"][k])
            elif k > 0:
                arrive([state["bx"][4 - k]])
            if step < 3:
                state["b"][k] = [
                    copy(block(k, -step), block(k, -step), at(0, 0, 0, 1)),
                    copy(block(k, step), block(k, step), at(0, 0, 0, -1)),
                ]
            elif step == 3:
                state["b"][k] = [
                    copy(half(k, -3, 0), half(k, -3, 0), at(0, 0, 0, 1)),
                    copy(half(k, 3, 1), half(k, 3, 1), at(0, 0, 0, -1)),
                ]

    def side_core(*ds):
        for d in ds:
            a = side.at[:, (z + d) % 8, core]
            state["core"].append(copy(a, a, at(0, 1, 0)))

    def panel_rows(c, t):
        def rows(o):
            parts = []
            for u in range(4):
                place = (c // 4, 2 * (c % 4) + u // 2, u % 2)
                parts.append(main[(*place, pl.ds(LONG_AT[t] + o, LONG[t] // 3, stride=3), slice(None))])
                parts.append(side[(*place, pl.ds(SHORT_AT[t] + o, SHORT[t] // 3, stride=3), slice(None))])
            return jnp.concatenate(parts, axis=0)

        return rows

    def app_tile(n, place):
        unflatten(lambda o: app[n, pl.ds(o, 96, stride=3), :], place)

    live = [my_row > panel + t for t in range(3)]
    rest = (1, 2, 3)
    agenda = {
        (0, 0): [lambda: other_core(1), lambda: other_core(2), row_start],
        (0, 1): [lambda: side_ring(1, *rest), lambda: side_core(0)],
        (0, 3): [lambda: main_ring(3), lambda: side_ring(3, 0)],
        (1, 0): [lambda: side_ring(2, *rest), lambda: side_core(-1, 1)],
        (1, 2): [lambda: main_ring(4), lambda: side_ring(4, 0)],
        (1, 3): [lambda: main_core(0, -1, 1)],
        (1, 5): [lambda: side_ring(3, *rest), lambda: side_core(-2, 2)],
        (2, 1): [lambda: main_core(-2, 2)],
        (2, 3): [lambda: main_core(-3, 3)],
        (2, 4): [lambda: side_ring(4, *rest), lambda: side_core(-3, 3, 4)],
    }

    send_quarters()
    pick_rows()
    quarters_ready()
    bulk_start()
    for i in range(3):
        gather(i)
    main_ring(1)
    side_ring(1, 0)
    side_ring(0, *rest)
    main_ring(2)
    side_ring(2, 0)
    placed(0)
    app_tile(0, bt.at[0, 0])
    for t in range(3):
        sa[:, 0:256] = load(bt.at[0, 0]) if t == 0 else load(g.at[t, t - 1])
        start_tile(sa)
        for blk in range(6):
            factor_block(sa, BLK * blk)
            for phase in agenda.get((t, blk), []):
                phase()
        finish_tile(sa, linv.at[t], lfac.at[t])
        if t == 0:
            placed(1)
            placed(2)
            for n, place in enumerate([(0, 0), (1, 0), (0, 1), (1, 1), (2, 1)]):
                app_tile(n + 1, g.at[place])
        panel_step(t, g, linv)
        if t == 1:
            row_ready()
            own_step(0, g, linv, live)
        if t > 0:
            own_step(t, g, linv, live)
    weights(g, linv, w, whi, wlo)
    tile = panel + which
    special_tile(special, flat, g, lfac, which, my_row == tile)
    take = jnp.logical_and(which < 3, my_row >= tile)
    main_core(4)
    arrive(state["core"])

    def one(c, carry):
        for i in range(4):
            convert(lambda t, i=i: panel_rows(4 * c + i, t), bt.at[i], bhi.at[i], blo.at[i])
        for i in range(4):
            j = 4 * (4 * c + i) + my_col
            update(4 * c + i, matrix, out, bhi.at[i], blo.at[i], whi, wlo, flat, j, panel, which, take)
        return carry

    lax.fori_loop(0, 4, one, 0)
    for c in sent:
        c.wait_send()
    quarters_sent()


def body(matrix, panel_index):
    flat = matrix.reshape(16, 288, 128)
    V = pltpu.VMEM
    scratch = [
        V((2, 4, 4, 9, 128), F32), V((4, 2, 4, 9, 128), F32), V((6, 9, 128), F32), V((8, 1, 9, 128), F32), V((8, 2, 9, 128), F32), V((8, 3, 9, 128), F32),
        V((2, 4, 4, 1, 9, 128), F32), V((2, 4, 4, 2, 9, 128), F32), V((2, 4, 4, 3, 9, 128), F32),
        V((4, 288, 128), F32), V((3, 288, 128), F32), V((6, 288, 128), F32), V((4, 72, 128), F32),
        V((4, 8, 2, sum(LONG), 128), F32), V((4, 8, 2, sum(SHORT), 128), F32),
        V((B, 512), F32), V((3, 256, 256), F32), V((3, B, 256), F32), V((3, 3, 2, 256, 128), F32),
        V((3, 2, B, 128), F32), V((B, 768), BF16), V((B, 768), BF16), V((4, 3, 2, B, 128), F32),
        V((4, B, 768), BF16), V((4, B, 768), BF16), V((2, B, 128), F32), V((288, 128), F32),
        pltpu.SemaphoreType.DMA((N_SEM,)), pltpu.SemaphoreType.DMA((N_SEM,)),
        pltpu.SemaphoreType.DMA((4,)), pltpu.SemaphoreType.DMA((4,)),
    ]
    out = pl.pallas_call(
        kernel,
        out_shape=jax.ShapeDtypeStruct((16, 288, 128), F32),
        in_specs=[pl.BlockSpec(memory_space=pltpu.SMEM), pl.BlockSpec(memory_space=pltpu.VMEM)],
        out_specs=pl.BlockSpec(memory_space=pltpu.VMEM),
        scratch_shapes=scratch,
        compiler_params=pltpu.CompilerParams(collective_id=0, has_side_effects=True, vmem_limit_bytes=48 << 20),
        name="panel_steps",
    )(panel_index, flat)
    return out.reshape(matrix.shape)


def solution(mesh):
    in_specs = (P(None, "row", None, "col", None), P())
    out_specs = P(None, "row", None, "col", None)
    return jax.shard_map(body, mesh=mesh, in_specs=in_specs, out_specs=out_specs, check_vma=False)
```

```python
import jax
import jax.numpy as jnp
from jax import lax
from jax.experimental import pallas as pl
from jax.experimental.pallas import tpu as pltpu
from jax.sharding import PartitionSpec as P

B = 192
BLK = 32
SUB = 16
HIGH = lax.Precision.HIGHEST
F32 = jnp.float32
BF16 = jnp.bfloat16


def lanes_below(n, shape):
    return lax.broadcasted_iota(jnp.int32, shape, 1) < n


def unflatten(get, dst):
    f0, f1, f2 = get(0), get(1), get(2)
    low = lanes_below(64, f0.shape)
    zero = jnp.zeros_like(f0)
    dst[0, pl.ds(0, 96, stride=2), :] = f0
    dst[1, pl.ds(0, 96, stride=2), :] = jnp.where(low, f1, zero)
    dst[0, pl.ds(1, 96, stride=2), :] = pltpu.roll(jnp.where(low, f2, f1), 64, 1)
    dst[1, pl.ds(1, 96, stride=2), :] = jnp.where(low, pltpu.roll(f2, 64, 1), zero)


def load(ref, rows=B):
    return jnp.concatenate([ref[0, 0:rows, :], ref[1, 0:rows, :]], axis=1)


def store(ref, value):
    ref[0, 0:B, :] = value[:, :128]
    ref[1, 0:B, :] = value[:, 128:]


def flatten(even, odd):
    e0, e1 = even[:, :128], even[:, 128:]
    o0, o1 = odd[:, :128], odd[:, 128:]
    low = lanes_below(64, e0.shape)
    return e0, jnp.where(low, e1, pltpu.roll(o0, 64, 1)), pltpu.roll(jnp.where(low, o1, o0), 64, 1)


def split3(u):
    h = u.astype(BF16)
    rest = u - h.astype(F32)
    m = rest.astype(BF16)
    return h, m, (rest - m.astype(F32)).astype(BF16)


def split2(u):
    h = u.astype(BF16)
    return h, (u - h.astype(F32)).astype(BF16)


def factor_block(sa, r0):
    lo = 128 * (r0 // 128)
    hi = 384 if r0 + BLK <= 128 else 512
    width = hi - lo
    tiles = width // 128
    rows = sa[r0:r0 + BLK, lo:hi]
    diag = jnp.ones((BLK, 128), F32)
    ids = lax.broadcasted_iota(jnp.int32, (BLK, 128), 0)
    for sub in range(BLK // SUB):
        top = sub * SUB
        height = BLK - top
        live = rows[top:, :]
        col0 = r0 + top - lo
        cols = [jnp.broadcast_to(live[:, col0 + i:col0 + i + 1], (height, 128)) for i in range(SUB)]
        sub_ids = lax.broadcasted_iota(jnp.int32, (height, 128), 0)
        for j in range(SUB):
            cj = cols[j]
            pivot = cj[j:j + 1, :]
            f = jnp.where(sub_ids > j, cj * (1.0 / pivot), 0.0)
            diag = jnp.where(ids == top + j, pivot, diag)
            for i in range(j + 1, SUB):
                cols[i] = cols[i] - f * cj[i:i + 1, :]
            wide = jnp.concatenate([f] * tiles, axis=1)
            live = live - wide * live[j:j + 1, :]
        rows = live if top == 0 else jnp.concatenate([rows[:top], live], axis=0)
    u = rows * jnp.concatenate([lax.rsqrt(diag)] * tiles, axis=1)
    sa[r0:r0 + BLK, lo:hi] = u
    if r0 + BLK < B:
        h, m, l = split3(u)
        left = jnp.concatenate([h, h, m, h, m, l], axis=0)[:, :256 - lo]
        right = jnp.concatenate([h, m, h, l, m, h], axis=0)
        change = lax.dot_general(left, right, (((0,), (0,)), ((), ())), preferred_element_type=F32)
        sa[r0 + BLK:B, lo:hi] = sa[r0 + BLK:B, lo:hi] - change[r0 + BLK - lo:B - lo]


def start_tile(sa):
    r = lax.broadcasted_iota(jnp.int32, (B, 256), 0)
    c = lax.broadcasted_iota(jnp.int32, (B, 256), 1)
    sa[:, 256:512] = jnp.where(r == c, 1.0, 0.0).astype(F32)


def finish_tile(sa, linv, lfac):
    r = lax.broadcasted_iota(jnp.int32, (B, 256), 0)
    c = lax.broadcasted_iota(jnp.int32, (B, 256), 1)
    linv[0:B, :] = sa[:, 256:512]
    linv[B:256, :] = jnp.zeros((256 - B, 256), F32)
    u = jnp.where(r <= c, sa[:, 0:256], 0.0)
    full = jnp.concatenate([u, jnp.zeros((64, 256), F32)], axis=0)
    lfac[...] = full.T[0:B, :]


def nt(a, b):
    return lax.dot_general(a, b, (((1,), (1,)), ((), ())), precision=HIGH, preferred_element_type=F32)


def nn(a, b):
    return jnp.dot(a, b, precision=HIGH, preferred_element_type=F32)


def panel_step(t, g, linv):
    for p in range(t, 2):
        store(g.at[t, p], nt(load(g.at[t, p]), linv[t]))
    for s in range(t + 1, 3):
        for p in range(s - 1, 2):
            store(g.at[s, p], load(g.at[s, p]) - nt(load(g.at[t, p]), load(g.at[t, s - 1], 256)))


def own_step(t, g, linv, live):
    v = jnp.where(live[t], nt(load(g.at[t, 2]), linv[t]), 0.0)
    store(g.at[t, 2], v)
    for s in range(t + 1, 3):
        store(g.at[s, 2], load(g.at[s, 2]) - nt(v, load(g.at[t, s - 1], 256)))


def weights(g, linv, w, whi, wlo):
    def full(t, p):
        return load(g.at[t, p], 256)

    w2 = nn(load(g.at[2, 2]), linv[2])
    w1 = nn(load(g.at[1, 2]) - nn(w2, full(1, 1)), linv[1])
    w0 = nn(load(g.at[0, 2]) - nn(w2, full(0, 1)) - nn(w1, full(0, 0)), linv[0])
    for t, v in enumerate((w0, w1, w2)):
        store(w.at[t], v)
    for half in range(2):
        v = jnp.concatenate([w[i // 2, i % 2, pl.ds(half, 96, stride=2), :] for i in range(6)], axis=1)
        whi[96 * half:96 * half + 96, :], wlo[96 * half:96 * half + 96, :] = split2(v)


def special_tile(special, flat, g, lfac, which, same):
    x = jnp.where(which == 0, load(g.at[0, 2]), jnp.where(which == 1, load(g.at[1, 2]), load(g.at[2, 2])))
    f = jnp.where(which == 0, lfac[0], jnp.where(which == 1, lfac[1], lfac[2]))
    store(special, jnp.where(same, f, x))
    even = jnp.concatenate([special[i, pl.ds(0, 96, stride=2), :] for i in range(2)], axis=1)
    odd = jnp.concatenate([special[i, pl.ds(1, 96, stride=2), :] for i in range(2)], axis=1)
    for i, v in enumerate(flatten(even, odd)):
        flat[pl.ds(i, 96, stride=3), :] = v


def convert(rows, bt, bhi, blo):
    for t in range(3):
        unflatten(rows(t), bt.at[t])
    bhi[...], blo[...] = split2(jnp.concatenate([bt[i // 2, i % 2] for i in range(6)], axis=1))


def update(c, matrix, out, bhi, blo, whi, wlo, flat, j, panel, which, take):
    dims = (((1,), (1,)), ((), ()))
    both = lax.dot_general(jnp.concatenate([whi[...], wlo[...]], axis=0), bhi[...], dims, preferred_element_type=F32)
    change = both[:B] + both[B:] + lax.dot_general(whi[...], blo[...], dims, preferred_element_type=F32)
    change = jnp.concatenate([change, jnp.zeros((B, 64), F32)], axis=1)
    change = jnp.where(j > panel, change, 0.0)
    use = jnp.logical_and(take, j == panel + which)
    for i, v in enumerate(flatten(change[0:96], change[96:192])):
        old = matrix[c, pl.ds(i, 96, stride=3), :]
        out[c, pl.ds(i, 96, stride=3), :] = jnp.where(use, flat[pl.ds(i, 96, stride=3), :], old - v)


MESH = pl.DeviceIdType.MESH
N_SEM = 256
ORDER = [(0, 0), (1, 0), (1, 1), (2, 0), (2, 1), (2, 2)]
GROUPS = [(0, 1), (1, 2), (3, 3)]
LONG, SHORT = (48, 48, 48), (24, 24, 24)
LONG_AT, SHORT_AT = (0, 48, 96), (0, 24, 48)


def kernel(
    panel_ref, matrix, out,
    cut, got, pick, gotz0, gotz1, gotz2, tile0, tile1, tile2, rel, own, app, fresh, main, side,
    sa, linv, lfac, g, w, whi, wlo, bt, bhi, blo, special, flat,
    send_sem, recv_sem, quarter_sem, fresh_sem,
):
    panel = panel_ref[0]
    my_row, my_col = lax.axis_index("row"), lax.axis_index("col")
    x, core = lax.div(my_row, 16), lax.rem(my_row, 2)
    z = lax.rem(lax.div(my_row, 2), 8)
    xs = [x] + [lax.rem(x + d, 4) for d in range(1, 4)]
    ys = [my_col] + [lax.rem(my_col + d, 4) for d in range(1, 4)]
    zs = [z] + [lax.rem(z + d, 8) for d in range(1, 8)]
    cs = [core, 1 - core]
    x_rows, z_rows = [16 * v for v in xs], [2 * v for v in zs]
    known = {}
    here = lax.rem(my_row, 4)
    which = lax.rem(my_col - panel + 64, 4)
    gathered = [tile0, tile1, tile2]
    gotz = [gotz0, gotz1, gotz2]

    def at(dx, dc, dy, dz=0):
        key = (dx, dc, dy, dz % 8)
        if key not in known:
            known[key] = {"row": x_rows[dx] + z_rows[dz % 8] + cs[dc], "col": ys[dy]}
        return known[key]

    def at_quarter(u):
        return {"row": my_row - here + u, "col": here}

    group = [(dx, dc, dy) for dc in range(2) for dx in range(4) for dy in range(4)][1:]
    count = [0]
    sent = []

    def copy(src, dst, device):
        i = count[0]
        count[0] += 1
        c = pltpu.make_async_remote_copy(
            src_ref=src, dst_ref=dst, send_sem=send_sem.at[i], recv_sem=recv_sem.at[i],
            device_id=device, device_id_type=MESH,
        )
        c.start()
        sent.append(c)
        return c

    def arrive(copies):
        for c in copies:
            c.wait_recv()

    barrier = pltpu.get_barrier_semaphore()
    near = [at(*d) for d in group] + [at(0, 0, 0, dz) for dz in range(1, 8)]
    z_half = lax.rem(z, 2)
    across = z + 1 - 2 * z_half
    for dc in range(2):
        for dy in range(4):
            if dc or dy:
                near.append({"row": x_rows[0] + 2 * across + cs[dc], "col": ys[dy]})
    for device in near:
        pl.semaphore_signal(barrier, inc=1, device_id=device, device_id_type=MESH)

    g[...] = jnp.zeros_like(g)
    slot = jnp.minimum((panel + which) // 4, 15)
    mine = matrix[slot]
    rel[0] = mine
    for i in range(32):
        cut[i // 16, (i // 4) % 4, i % 4] = mine[9 * i:9 * i + 9]
    got[x, core, my_col] = cut[core, x, my_col]
    pl.semaphore_wait(barrier, len(near))

    pieces = []
    for dx, dc, dy in group:
        pieces.append(copy(
            cut.at[cs[dc], xs[dx], ys[dy]], got.at[x, core, my_col], at(dx, dc, dy),
        ))
    state = {}
    to_me = here == my_col
    quarters = []

    def send_quarters():
        for d in range(4):
            u = lax.rem(here + d, 4)
            part = rel.at[0, pl.ds(pl.multiple_of(72 * u, 8), 72)]
            quarters.append(pltpu.make_async_remote_copy(
                src_ref=part, dst_ref=fresh.at[my_col], send_sem=quarter_sem.at[d], recv_sem=fresh_sem.at[my_col],
                device_id=at_quarter(u), device_id_type=MESH,
            ))
        for c in quarters[1:]:
            c.start()

        @pl.when(jnp.logical_not(to_me))
        def _():
            quarters[0].start()

        @pl.when(to_me)
        def _():
            fresh[my_col] = rel[0, pl.ds(pl.multiple_of(72 * here, 8), 72), :]

    def quarters_ready():
        for q in range(4):
            c = pltpu.make_async_remote_copy(
                src_ref=rel.at[0, pl.ds(0, 72)], dst_ref=fresh.at[q], send_sem=quarter_sem.at[0], recv_sem=fresh_sem.at[q],
                device_id=at_quarter(0), device_id_type=MESH,
            )

            @pl.when(jnp.logical_not(jnp.logical_and(to_me, my_col == q)))
            def _():
                c.wait_recv()

    def quarters_sent():
        for c in quarters[1:]:
            c.wait_send()

        @pl.when(jnp.logical_not(to_me))
        def _():
            quarters[0].wait_send()

    def pick_rows():
        arrive(pieces)
        for n, (s, t) in enumerate(ORDER):
            r = panel + s
            pick[n] = got[r // 16, r % 2, (panel + t) % 4]
        state["z"] = []
        for (a, n), dst in zip(GROUPS, gotz):
            dst[z] = pick[a:a + n]
            state["z"].append([copy(pick.at[pl.ds(a, n)], dst.at[z], at(0, 0, 0, dz)) for dz in range(1, 8)])

    def gather(i):
        arrive(state["z"][i])
        a, n = GROUPS[i]
        tile = gathered[i]
        for m in range(n):
            r = panel + ORDER[a + m][0]
            tile[core, x, my_col, m] = gotz[i][(r // 2) % 8, m]
        mine = tile.at[core, x, my_col]
        members = group if i == 0 else [d for d in group if d[1] == 0]
        state[i] = [copy(mine, mine, at(*d)) for d in members]

    def other_core(i):
        arrive(state[i])
        half = gathered[i].at[core]
        state[i] = [copy(half, half, at(0, 1, 0))]

    def placed(i):
        arrive(state[i])
        a, n = GROUPS[i]
        for m in range(n):
            for p in range(32):
                app[a + m, 9 * p:9 * p + 9, :] = gathered[i][p // 16, (p // 4) % 4, p % 4, m]

    def row_start():
        state["y"] = [copy(rel.at[0], rel.at[d], at(0, 0, d)) for d in range(1, 4)]

    def row_ready():
        arrive(state["y"])
        for t in range(3):
            own[t] = rel[(my_col - panel - t + 64) % 4]
            unflatten(lambda o, t=t: own[t, pl.ds(o, 96, stride=3), :], g.at[t, 2])

    def main_block(d):
        return main.at[x, zs[d % 8], core]

    def pass_x(d):
        state["ax"][d] = [copy(main_block(d), main_block(d), at(k, 0, 0)) for k in range(1, 4)]

    def bulk_start():
        for t in range(3):
            v = fresh[(panel + t) % 4]
            main[x, z, core, LONG_AT[t]:LONG_AT[t] + LONG[t], :] = v[:LONG[t]]
            side[x, z, core, SHORT_AT[t]:SHORT_AT[t] + SHORT[t], :] = v[LONG[t]:]
        state["core"], state["ax"] = [], {}
        main_ring(0)
        b = side.at[x, z, core]
        state["b"] = {}
        state["bx"] = {d: copy(b, b, at(d, 0, 0)) for d in range(1, 4)}
        side_ring(0, 0)

    def main_ring(step):
        def part(d, h):
            return main.at[x, zs[d % 8], core, pl.ds(72 * h, 72)]

        if step > 0:
            arrive(state["a"])
        if step < 3:
            state["a"] = [
                copy(main_block(-step), main_block(-step), at(0, 0, 0, 1)),
                copy(main_block(step), main_block(step), at(0, 0, 0, -1)),
            ]
        elif step == 3:
            state["a"] = [
                copy(part(-3, 0), part(-3, 0), at(0, 0, 0, 1)), copy(part(3, 1), part(3, 1), at(0, 0, 0, -1)),
            ]
        for d in ([0] if step == 0 else [-step, step] if step < 4 else [4]):
            pass_x(d)

    def main_core(*ds):
        for d in ds:
            arrive(state["ax"][d])
            a = main.at[:, zs[d % 8], core]
            state["core"].append(copy(a, a, at(0, 1, 0)))

    def side_ring(step, *ks):
        def block(k, d):
            return side.at[xs[k], zs[d % 8], core]

        def half(k, d, h):
            return side.at[xs[k], zs[d % 8], core, pl.ds(40 * h, 40 - 8 * h)]

        for k in ks:
            if step > 0:
                arrive(state["b"][k])
            elif k > 0:
                arrive([state["bx"][4 - k]])
            if step < 3:
                state["b"][k] = [
                    copy(block(k, -step), block(k, -step), at(0, 0, 0, 1)),
                    copy(block(k, step), block(k, step), at(0, 0, 0, -1)),
                ]
            elif step == 3:
                state["b"][k] = [
                    copy(half(k, -3, 0), half(k, -3, 0), at(0, 0, 0, 1)),
                    copy(half(k, 3, 1), half(k, 3, 1), at(0, 0, 0, -1)),
                ]

    def side_core(*ds):
        for d in ds:
            a = side.at[:, zs[d % 8], core]
            state["core"].append(copy(a, a, at(0, 1, 0)))

    def panel_rows(c, t):
        def rows(o):
            parts = []
            for u in range(4):
                place = (c // 4, 2 * (c % 4) + u // 2, u % 2)
                parts.append(main[(*place, pl.ds(LONG_AT[t] + o, LONG[t] // 3, stride=3), slice(None))])
                parts.append(side[(*place, pl.ds(SHORT_AT[t] + o, SHORT[t] // 3, stride=3), slice(None))])
            return jnp.concatenate(parts, axis=0)

        return rows

    def app_tile(n, place):
        unflatten(lambda o: app[n, pl.ds(o, 96, stride=3), :], place)

    live = [my_row > panel + t for t in range(3)]
    rest = (1, 2, 3)
    agenda = {
        (0, 0): [lambda: other_core(1), lambda: other_core(2), row_start],
        (0, 1): [lambda: side_ring(1, *rest), lambda: side_core(0)],
        (0, 3): [lambda: main_ring(3), lambda: side_ring(3, 0)],
        (1, 1): [lambda: side_ring(2, *rest), lambda: side_core(-1, 1)],
        (1, 2): [lambda: main_ring(4), lambda: side_ring(4, 0)],
        (1, 4): [lambda: main_core(0, -1, 1)],
        (2, 2): [lambda: side_ring(3, *rest), lambda: side_core(-2, 2)],
        (2, 4): [lambda: main_core(-2, 2)],
    }

    send_quarters()
    pick_rows()
    quarters_ready()
    bulk_start()
    for i in range(3):
        gather(i)
    main_ring(1)
    side_ring(1, 0)
    side_ring(0, *rest)
    main_ring(2)
    side_ring(2, 0)
    placed(0)
    app_tile(0, bt.at[0, 0])
    for t in range(3):
        sa[:, 0:256] = load(bt.at[0, 0]) if t == 0 else load(g.at[t, t - 1])
        start_tile(sa)
        for blk in range(6):
            factor_block(sa, BLK * blk)
            for phase in agenda.get((t, blk), []):
                phase()
        finish_tile(sa, linv.at[t], lfac.at[t])
        if t == 0:
            placed(1)
            placed(2)
            for n, place in enumerate([(0, 0), (1, 0), (0, 1), (1, 1), (2, 1)]):
                app_tile(n + 1, g.at[place])
        panel_step(t, g, linv)
        if t == 1:
            row_ready()
            own_step(0, g, linv, live)
        if t > 0:
            own_step(t, g, linv, live)
    weights(g, linv, w, whi, wlo)
    tile = panel + which
    special_tile(special, flat, g, lfac, which, my_row == tile)
    take = jnp.logical_and(which < 3, my_row >= tile)
    main_core(-3, 3)
    side_ring(4, *rest)
    side_core(-3, 3, 4)
    main_core(4)
    for c in sent:
        c.wait_send()
    quarters_sent()
    arrive(state["core"])

    def one(c, carry):
        for i in range(4):
            convert(lambda t, i=i: panel_rows(4 * c + i, t), bt.at[i], bhi.at[i], blo.at[i])
        for i in range(4):
            j = 4 * (4 * c + i) + my_col
            update(4 * c + i, matrix, out, bhi.at[i], blo.at[i], whi, wlo, flat, j, panel, which, take)
        return carry

    lax.fori_loop(0, 4, one, 0)


def body(matrix, panel_index):
    flat = matrix.reshape(16, 288, 128)
    V = pltpu.VMEM
    scratch = [
        V((2, 4, 4, 9, 128), F32), V((4, 2, 4, 9, 128), F32), V((6, 9, 128), F32), V((8, 1, 9, 128), F32), V((8, 2, 9, 128), F32), V((8, 3, 9, 128), F32),
        V((2, 4, 4, 1, 9, 128), F32), V((2, 4, 4, 2, 9, 128), F32), V((2, 4, 4, 3, 9, 128), F32),
        V((4, 288, 128), F32), V((3, 288, 128), F32), V((6, 288, 128), F32), V((4, 72, 128), F32),
        V((4, 8, 2, sum(LONG), 128), F32), V((4, 8, 2, sum(SHORT), 128), F32),
        V((B, 512), F32), V((3, 256, 256), F32), V((3, B, 256), F32), V((3, 3, 2, 256, 128), F32),
        V((3, 2, B, 128), F32), V((B, 768), BF16), V((B, 768), BF16), V((4, 3, 2, B, 128), F32),
        V((4, B, 768), BF16), V((4, B, 768), BF16), V((2, B, 128), F32), V((288, 128), F32),
        pltpu.SemaphoreType.DMA((N_SEM,)), pltpu.SemaphoreType.DMA((N_SEM,)),
        pltpu.SemaphoreType.DMA((4,)), pltpu.SemaphoreType.DMA((4,)),
    ]
    out = pl.pallas_call(
        kernel,
        out_shape=jax.ShapeDtypeStruct((16, 288, 128), F32),
        in_specs=[pl.BlockSpec(memory_space=pltpu.SMEM), pl.BlockSpec(memory_space=pltpu.VMEM)],
        out_specs=pl.BlockSpec(memory_space=pltpu.VMEM),
        scratch_shapes=scratch,
        compiler_params=pltpu.CompilerParams(collective_id=0, has_side_effects=True, vmem_limit_bytes=48 << 20),
        name="panel_steps",
    )(panel_index, flat)
    return out.reshape(matrix.shape)


def solution(mesh):
    in_specs = (P(None, "row", None, "col", None), P())
    out_specs = P(None, "row", None, "col", None)
    return jax.shard_map(body, mesh=mesh, in_specs=in_specs, out_specs=out_specs, check_vma=False)
```

```python
import jax
import jax.numpy as jnp
from jax import lax
from jax.experimental import pallas as pl
from jax.experimental.pallas import tpu as pltpu
from jax.sharding import PartitionSpec as P

B = 192
BLK = 32
SUB = 16
HIGH = lax.Precision.HIGHEST
F32 = jnp.float32
BF16 = jnp.bfloat16


def lanes_below(n, shape):
    return lax.broadcasted_iota(jnp.int32, shape, 1) < n


def unflatten(get, dst):
    f0, f1, f2 = get(0), get(1), get(2)
    low = lanes_below(64, f0.shape)
    zero = jnp.zeros_like(f0)
    dst[0, pl.ds(0, 96, stride=2), :] = f0
    dst[1, pl.ds(0, 96, stride=2), :] = jnp.where(low, f1, zero)
    dst[0, pl.ds(1, 96, stride=2), :] = pltpu.roll(jnp.where(low, f2, f1), 64, 1)
    dst[1, pl.ds(1, 96, stride=2), :] = jnp.where(low, pltpu.roll(f2, 64, 1), zero)


def load(ref, rows=B):
    return jnp.concatenate([ref[0, 0:rows, :], ref[1, 0:rows, :]], axis=1)


def store(ref, value):
    ref[0, 0:B, :] = value[:, :128]
    ref[1, 0:B, :] = value[:, 128:]


def flatten(even, odd):
    e0, e1 = even[:, :128], even[:, 128:]
    o0, o1 = odd[:, :128], odd[:, 128:]
    low = lanes_below(64, e0.shape)
    return e0, jnp.where(low, e1, pltpu.roll(o0, 64, 1)), pltpu.roll(jnp.where(low, o1, o0), 64, 1)


def split3(u):
    h = u.astype(BF16)
    rest = u - h.astype(F32)
    m = rest.astype(BF16)
    return h, m, (rest - m.astype(F32)).astype(BF16)


def split2(u):
    h = u.astype(BF16)
    return h, (u - h.astype(F32)).astype(BF16)


def factor_block(sa, r0):
    lo = 128 * (r0 // 128)
    hi = 384 if r0 + BLK <= 128 else 512
    width = hi - lo
    tiles = width // 128
    rows = sa[r0:r0 + BLK, lo:hi]
    diag = jnp.ones((BLK, 128), F32)
    ids = lax.broadcasted_iota(jnp.int32, (BLK, 128), 0)
    for sub in range(BLK // SUB):
        top = sub * SUB
        height = BLK - top
        live = rows[top:, :]
        col0 = r0 + top - lo
        cols = [jnp.broadcast_to(live[:, col0 + i:col0 + i + 1], (height, 128)) for i in range(SUB)]
        sub_ids = lax.broadcasted_iota(jnp.int32, (height, 128), 0)
        for j in range(SUB):
            cj = cols[j]
            pivot = cj[j:j + 1, :]
            f = jnp.where(sub_ids > j, cj * (1.0 / pivot), 0.0)
            diag = jnp.where(ids == top + j, pivot, diag)
            for i in range(j + 1, SUB):
                cols[i] = cols[i] - f * cj[i:i + 1, :]
            wide = jnp.concatenate([f] * tiles, axis=1)
            live = live - wide * live[j:j + 1, :]
        rows = live if top == 0 else jnp.concatenate([rows[:top], live], axis=0)
    u = rows * jnp.concatenate([lax.rsqrt(diag)] * tiles, axis=1)
    sa[r0:r0 + BLK, lo:hi] = u
    if r0 + BLK < B:
        h, m, l = split3(u)
        left = jnp.concatenate([h, h, m, h, m, l], axis=0)[:, :256 - lo]
        right = jnp.concatenate([h, m, h, l, m, h], axis=0)
        change = lax.dot_general(left, right, (((0,), (0,)), ((), ())), preferred_element_type=F32)
        sa[r0 + BLK:B, lo:hi] = sa[r0 + BLK:B, lo:hi] - change[r0 + BLK - lo:B - lo]


def start_tile(sa):
    r = lax.broadcasted_iota(jnp.int32, (B, 256), 0)
    c = lax.broadcasted_iota(jnp.int32, (B, 256), 1)
    sa[:, 256:512] = jnp.where(r == c, 1.0, 0.0).astype(F32)


def finish_tile(sa, linv, lfac):
    r = lax.broadcasted_iota(jnp.int32, (B, 256), 0)
    c = lax.broadcasted_iota(jnp.int32, (B, 256), 1)
    linv[0:B, :] = sa[:, 256:512]
    linv[B:256, :] = jnp.zeros((256 - B, 256), F32)
    u = jnp.where(r <= c, sa[:, 0:256], 0.0)
    full = jnp.concatenate([u, jnp.zeros((64, 256), F32)], axis=0)
    lfac[...] = full.T[0:B, :]


def nt(a, b):
    return lax.dot_general(a, b, (((1,), (1,)), ((), ())), precision=HIGH, preferred_element_type=F32)


def nn(a, b):
    return jnp.dot(a, b, precision=HIGH, preferred_element_type=F32)


def panel_step(t, g, linv):
    for p in range(t, 2):
        store(g.at[t, p], nt(load(g.at[t, p]), linv[t]))
    for s in range(t + 1, 3):
        for p in range(s - 1, 2):
            store(g.at[s, p], load(g.at[s, p]) - nt(load(g.at[t, p]), load(g.at[t, s - 1], 256)))


def own_step(t, g, linv, live):
    v = jnp.where(live[t], nt(load(g.at[t, 2]), linv[t]), 0.0)
    store(g.at[t, 2], v)
    for s in range(t + 1, 3):
        store(g.at[s, 2], load(g.at[s, 2]) - nt(v, load(g.at[t, s - 1], 256)))


def weights(g, linv, w, whi, wlo):
    def full(t, p):
        return load(g.at[t, p], 256)

    w2 = nn(load(g.at[2, 2]), linv[2])
    w1 = nn(load(g.at[1, 2]) - nn(w2, full(1, 1)), linv[1])
    w0 = nn(load(g.at[0, 2]) - nn(w2, full(0, 1)) - nn(w1, full(0, 0)), linv[0])
    for t, v in enumerate((w0, w1, w2)):
        store(w.at[t], v)
    for half in range(2):
        v = jnp.concatenate([w[i // 2, i % 2, pl.ds(half, 96, stride=2), :] for i in range(6)], axis=1)
        whi[96 * half:96 * half + 96, :], wlo[96 * half:96 * half + 96, :] = split2(v)


def special_tile(special, flat, g, lfac, which, same):
    x = jnp.where(which == 0, load(g.at[0, 2]), jnp.where(which == 1, load(g.at[1, 2]), load(g.at[2, 2])))
    f = jnp.where(which == 0, lfac[0], jnp.where(which == 1, lfac[1], lfac[2]))
    store(special, jnp.where(same, f, x))
    even = jnp.concatenate([special[i, pl.ds(0, 96, stride=2), :] for i in range(2)], axis=1)
    odd = jnp.concatenate([special[i, pl.ds(1, 96, stride=2), :] for i in range(2)], axis=1)
    for i, v in enumerate(flatten(even, odd)):
        flat[pl.ds(i, 96, stride=3), :] = v


def convert(rows, bt, bhi, blo):
    for t in range(3):
        unflatten(rows(t), bt.at[t])
    bhi[...], blo[...] = split2(jnp.concatenate([bt[i // 2, i % 2] for i in range(6)], axis=1))


def update(c, matrix, out, bhi, blo, whi, wlo, flat, j, panel, which, take):
    dims = (((1,), (1,)), ((), ()))
    both = lax.dot_general(jnp.concatenate([whi[...], wlo[...]], axis=0), bhi[...], dims, preferred_element_type=F32)
    change = both[:B] + both[B:] + lax.dot_general(whi[...], blo[...], dims, preferred_element_type=F32)
    change = jnp.concatenate([change, jnp.zeros((B, 64), F32)], axis=1)
    change = jnp.where(j > panel, change, 0.0)
    use = jnp.logical_and(take, j == panel + which)
    for i, v in enumerate(flatten(change[0:96], change[96:192])):
        old = matrix[c, pl.ds(i, 96, stride=3), :]
        out[c, pl.ds(i, 96, stride=3), :] = jnp.where(use, flat[pl.ds(i, 96, stride=3), :], old - v)


MESH = pl.DeviceIdType.MESH
N_SEM = 256
ORDER = [(0, 0), (1, 0), (1, 1), (2, 0), (2, 1), (2, 2)]
GROUPS = [(0, 1), (1, 5)]
LONG, SHORT = (48, 48, 48), (24, 24, 24)
LONG_AT, SHORT_AT = (0, 48, 96), (0, 24, 48)


def kernel(
    panel_ref, matrix, out,
    cut, got, pick, gotz0, gotz1, tile0, tile1, rel, own, app, fresh, main, side,
    sa, linv, lfac, g, w, whi, wlo, bt, bhi, blo, special, flat,
    send_sem, recv_sem, quarter_sem, fresh_sem,
):
    panel = panel_ref[0]
    my_row, my_col = lax.axis_index("row"), lax.axis_index("col")
    x, core = lax.div(my_row, 16), lax.rem(my_row, 2)
    z = lax.rem(lax.div(my_row, 2), 8)
    xs = [x] + [lax.rem(x + d, 4) for d in range(1, 4)]
    ys = [my_col] + [lax.rem(my_col + d, 4) for d in range(1, 4)]
    zs = [z] + [lax.rem(z + d, 8) for d in range(1, 8)]
    cs = [core, 1 - core]
    x_rows, z_rows = [16 * v for v in xs], [2 * v for v in zs]
    known = {}
    here = lax.rem(my_row, 4)
    which = lax.rem(my_col - panel + 64, 4)
    gathered = [tile0, tile1]
    gotz = [gotz0, gotz1]

    def at(dx, dc, dy, dz=0):
        key = (dx, dc, dy, dz % 8)
        if key not in known:
            known[key] = {"row": x_rows[dx] + z_rows[dz % 8] + cs[dc], "col": ys[dy]}
        return known[key]

    def at_quarter(u):
        return {"row": my_row - here + u, "col": here}

    group = [(dx, dc, dy) for dc in range(2) for dx in range(4) for dy in range(4)][1:]
    count = [0]
    sent = []

    def copy(src, dst, device):
        i = count[0]
        count[0] += 1
        c = pltpu.make_async_remote_copy(
            src_ref=src, dst_ref=dst, send_sem=send_sem.at[i], recv_sem=recv_sem.at[i],
            device_id=device, device_id_type=MESH,
        )
        c.start()
        sent.append(c)
        return c

    def arrive(copies):
        for c in copies:
            c.wait_recv()

    barrier = pltpu.get_barrier_semaphore()
    near = [at(*d) for d in group] + [at(0, 0, 0, dz) for dz in range(1, 8)]
    z_half = lax.rem(z, 2)
    across = z + 1 - 2 * z_half
    for dc in range(2):
        for dy in range(4):
            if dc or dy:
                near.append({"row": x_rows[0] + 2 * across + cs[dc], "col": ys[dy]})
    for device in near:
        pl.semaphore_signal(barrier, inc=1, device_id=device, device_id_type=MESH)

    g[...] = jnp.zeros_like(g)
    slot = jnp.minimum((panel + which) // 4, 15)
    mine = matrix[slot]
    rel[0] = mine
    for i in range(32):
        cut[i // 16, (i // 4) % 4, i % 4] = mine[9 * i:9 * i + 9]
    got[x, core, my_col] = cut[core, x, my_col]
    pl.semaphore_wait(barrier, len(near))

    pieces = []
    for dx, dc, dy in group:
        pieces.append(copy(
            cut.at[cs[dc], xs[dx], ys[dy]], got.at[x, core, my_col], at(dx, dc, dy),
        ))
    state = {}
    to_me = here == my_col
    quarters = []

    def send_quarters():
        for d in range(4):
            u = lax.rem(here + d, 4)
            part = rel.at[0, pl.ds(pl.multiple_of(72 * u, 8), 72)]
            quarters.append(pltpu.make_async_remote_copy(
                src_ref=part, dst_ref=fresh.at[my_col], send_sem=quarter_sem.at[d], recv_sem=fresh_sem.at[my_col],
                device_id=at_quarter(u), device_id_type=MESH,
            ))
        for c in quarters[1:]:
            c.start()

        @pl.when(jnp.logical_not(to_me))
        def _():
            quarters[0].start()

        @pl.when(to_me)
        def _():
            fresh[my_col] = rel[0, pl.ds(pl.multiple_of(72 * here, 8), 72), :]

    def quarters_ready():
        for q in range(4):
            c = pltpu.make_async_remote_copy(
                src_ref=rel.at[0, pl.ds(0, 72)], dst_ref=fresh.at[q], send_sem=quarter_sem.at[0], recv_sem=fresh_sem.at[q],
                device_id=at_quarter(0), device_id_type=MESH,
            )

            @pl.when(jnp.logical_not(jnp.logical_and(to_me, my_col == q)))
            def _():
                c.wait_recv()

    def quarters_sent():
        for c in quarters[1:]:
            c.wait_send()

        @pl.when(jnp.logical_not(to_me))
        def _():
            quarters[0].wait_send()

    def pick_rows():
        arrive(pieces)
        for n, (s, t) in enumerate(ORDER):
            r = panel + s
            pick[n] = got[r // 16, r % 2, (panel + t) % 4]
        state["z"] = []
        for (a, n), dst in zip(GROUPS, gotz):
            dst[z] = pick[a:a + n]
            state["z"].append([copy(pick.at[pl.ds(a, n)], dst.at[z], at(0, 0, 0, dz)) for dz in range(1, 8)])

    def gather(i):
        arrive(state["z"][i])
        a, n = GROUPS[i]
        tile = gathered[i]
        for m in range(n):
            r = panel + ORDER[a + m][0]
            tile[core, x, my_col, m] = gotz[i][(r // 2) % 8, m]
        mine = tile.at[core, x, my_col]
        members = [d for d in group if d[1] == 0 and (i == 0 or d[2] == 0)]
        state[i] = [copy(mine, mine, at(*d)) for d in members]

    def rest_y():
        arrive(state[1])
        line = tile1.at[core, :, my_col]
        state[1] = [copy(line, line, at(0, 0, d)) for d in range(1, 4)]

    def other_core(i):
        arrive(state[i])
        half = gathered[i].at[core]
        state[i] = [copy(half, half, at(0, 1, 0))]

    def placed(i):
        arrive(state[i])
        a, n = GROUPS[i]
        for m in range(n):
            for p in range(32):
                app[a + m, 9 * p:9 * p + 9, :] = gathered[i][p // 16, (p // 4) % 4, p % 4, m]

    def row_start():
        state["y"] = [copy(rel.at[0], rel.at[d], at(0, 0, d)) for d in range(1, 4)]

    def row_ready():
        arrive(state["y"])
        for t in range(3):
            own[t] = rel[(my_col - panel - t + 64) % 4]
            unflatten(lambda o, t=t: own[t, pl.ds(o, 96, stride=3), :], g.at[t, 2])

    def main_block(d):
        return main.at[x, zs[d % 8], core]

    def pass_x(d):
        state["ax"][d] = [copy(main_block(d), main_block(d), at(k, 0, 0)) for k in range(1, 4)]

    def bulk_start():
        for t in range(3):
            v = fresh[(panel + t) % 4]
            main[x, z, core, LONG_AT[t]:LONG_AT[t] + LONG[t], :] = v[:LONG[t]]
            side[x, z, core, SHORT_AT[t]:SHORT_AT[t] + SHORT[t], :] = v[LONG[t]:]
        state["core"], state["ax"] = [], {}
        main_ring(0)
        b = side.at[x, z, core]
        state["b"] = {}
        state["bx"] = {d: copy(b, b, at(d, 0, 0)) for d in range(1, 4)}
        side_ring(0, 0)

    def main_ring(step):
        def part(d, h):
            return main.at[x, zs[d % 8], core, pl.ds(72 * h, 72)]

        if step > 0:
            arrive(state["a"])
        if step < 3:
            state["a"] = [
                copy(main_block(-step), main_block(-step), at(0, 0, 0, 1)),
                copy(main_block(step), main_block(step), at(0, 0, 0, -1)),
            ]
        elif step == 3:
            state["a"] = [
                copy(part(-3, 0), part(-3, 0), at(0, 0, 0, 1)), copy(part(3, 1), part(3, 1), at(0, 0, 0, -1)),
            ]
        for d in ([0] if step == 0 else [-step, step] if step < 4 else [4]):
            pass_x(d)

    def main_core(*ds):
        for d in ds:
            arrive(state["ax"][d])
            a = main.at[:, zs[d % 8], core]
            state["core"].append(copy(a, a, at(0, 1, 0)))

    def side_ring(step, *ks):
        def block(k, d):
            return side.at[xs[k], zs[d % 8], core]

        def half(k, d, h):
            return side.at[xs[k], zs[d % 8], core, pl.ds(40 * h, 40 - 8 * h)]

        for k in ks:
            if step > 0:
                arrive(state["b"][k])
            elif k > 0:
                arrive([state["bx"][4 - k]])
            if step < 3:
                state["b"][k] = [
                    copy(block(k, -step), block(k, -step), at(0, 0, 0, 1)),
                    copy(block(k, step), block(k, step), at(0, 0, 0, -1)),
                ]
            elif step == 3:
                state["b"][k] = [
                    copy(half(k, -3, 0), half(k, -3, 0), at(0, 0, 0, 1)),
                    copy(half(k, 3, 1), half(k, 3, 1), at(0, 0, 0, -1)),
                ]

    def side_core(*ds):
        for d in ds:
            a = side.at[:, zs[d % 8], core]
            state["core"].append(copy(a, a, at(0, 1, 0)))

    def panel_rows(c, t):
        def rows(o):
            parts = []
            for u in range(4):
                place = (c // 4, 2 * (c % 4) + u // 2, u % 2)
                parts.append(main[(*place, pl.ds(LONG_AT[t] + o, LONG[t] // 3, stride=3), slice(None))])
                parts.append(side[(*place, pl.ds(SHORT_AT[t] + o, SHORT[t] // 3, stride=3), slice(None))])
            return jnp.concatenate(parts, axis=0)

        return rows

    def app_tile(n, place):
        unflatten(lambda o: app[n, pl.ds(o, 96, stride=3), :], place)

    live = [my_row > panel + t for t in range(3)]
    rest = (1, 2, 3)
    agenda = {
        (0, 0): [lambda: main_ring(2), lambda: side_ring(2, 0), row_start],
        (0, 1): [lambda: side_ring(1, *rest), lambda: side_core(0)],
        (0, 4): [lambda: main_ring(3), lambda: side_ring(3, 0)],
        (0, 5): [lambda: other_core(1)],
        (1, 1): [lambda: side_ring(2, *rest), lambda: side_core(-1, 1)],
        (1, 2): [lambda: main_ring(4), lambda: side_ring(4, 0)],
        (1, 4): [lambda: main_core(0, -1, 1)],
        (2, 2): [lambda: side_ring(3, *rest), lambda: side_core(-2, 2)],
        (2, 4): [lambda: main_core(-2, 2)],
    }

    send_quarters()
    pick_rows()
    quarters_ready()
    bulk_start()
    gather(0)
    gather(1)
    main_ring(1)
    side_ring(1, 0)
    rest_y()
    side_ring(0, *rest)
    other_core(0)
    placed(0)
    app_tile(0, bt.at[0, 0])
    for t in range(3):
        sa[:, 0:256] = load(bt.at[0, 0]) if t == 0 else load(g.at[t, t - 1])
        start_tile(sa)
        for blk in range(6):
            factor_block(sa, BLK * blk)
            for phase in agenda.get((t, blk), []):
                phase()
        finish_tile(sa, linv.at[t], lfac.at[t])
        if t == 0:
            placed(1)
            for n, place in enumerate([(0, 0), (1, 0), (0, 1), (1, 1), (2, 1)]):
                app_tile(n + 1, g.at[place])
        panel_step(t, g, linv)
        if t == 1:
            row_ready()
            own_step(0, g, linv, live)
        if t > 0:
            own_step(t, g, linv, live)
    weights(g, linv, w, whi, wlo)
    tile = panel + which
    special_tile(special, flat, g, lfac, which, my_row == tile)
    take = jnp.logical_and(which < 3, my_row >= tile)
    main_core(-3, 3)
    side_ring(4, *rest)
    side_core(-3, 3, 4)
    main_core(4)
    for c in sent:
        c.wait_send()
    quarters_sent()
    arrive(state["core"])

    def one(c, carry):
        for i in range(4):
            convert(lambda t, i=i: panel_rows(4 * c + i, t), bt.at[i], bhi.at[i], blo.at[i])
        for i in range(4):
            j = 4 * (4 * c + i) + my_col
            update(4 * c + i, matrix, out, bhi.at[i], blo.at[i], whi, wlo, flat, j, panel, which, take)
        return carry

    lax.fori_loop(0, 4, one, 0)


def body(matrix, panel_index):
    flat = matrix.reshape(16, 288, 128)
    V = pltpu.VMEM
    scratch = [
        V((2, 4, 4, 9, 128), F32), V((4, 2, 4, 9, 128), F32), V((6, 9, 128), F32), V((8, 1, 9, 128), F32), V((8, 5, 9, 128), F32),
        V((2, 4, 4, 1, 9, 128), F32), V((2, 4, 4, 5, 9, 128), F32),
        V((4, 288, 128), F32), V((3, 288, 128), F32), V((6, 288, 128), F32), V((4, 72, 128), F32),
        V((4, 8, 2, sum(LONG), 128), F32), V((4, 8, 2, sum(SHORT), 128), F32),
        V((B, 512), F32), V((3, 256, 256), F32), V((3, B, 256), F32), V((3, 3, 2, 256, 128), F32),
        V((3, 2, B, 128), F32), V((B, 768), BF16), V((B, 768), BF16), V((4, 3, 2, B, 128), F32),
        V((4, B, 768), BF16), V((4, B, 768), BF16), V((2, B, 128), F32), V((288, 128), F32),
        pltpu.SemaphoreType.DMA((N_SEM,)), pltpu.SemaphoreType.DMA((N_SEM,)),
        pltpu.SemaphoreType.DMA((4,)), pltpu.SemaphoreType.DMA((4,)),
    ]
    out = pl.pallas_call(
        kernel,
        out_shape=jax.ShapeDtypeStruct((16, 288, 128), F32),
        in_specs=[pl.BlockSpec(memory_space=pltpu.SMEM), pl.BlockSpec(memory_space=pltpu.VMEM)],
        out_specs=pl.BlockSpec(memory_space=pltpu.VMEM),
        scratch_shapes=scratch,
        compiler_params=pltpu.CompilerParams(collective_id=0, has_side_effects=True, vmem_limit_bytes=48 << 20),
        name="panel_steps",
    )(panel_index, flat)
    return out.reshape(matrix.shape)


def solution(mesh):
    in_specs = (P(None, "row", None, "col", None), P())
    out_specs = P(None, "row", None, "col", None)
    return jax.shard_map(body, mesh=mesh, in_specs=in_specs, out_specs=out_specs, check_vma=False)
```

```python
import jax
import jax.numpy as jnp
from jax import lax
from jax.experimental import pallas as pl
from jax.experimental.pallas import tpu as pltpu
from jax.sharding import PartitionSpec as P

B = 192
BLK = 32
SUB = 16
HIGH = lax.Precision.HIGHEST
F32 = jnp.float32
BF16 = jnp.bfloat16


def lanes_below(n, shape):
    return lax.broadcasted_iota(jnp.int32, shape, 1) < n


def unflatten(get, dst):
    f0, f1, f2 = get(0), get(1), get(2)
    low = lanes_below(64, f0.shape)
    zero = jnp.zeros_like(f0)
    dst[0, pl.ds(0, 96, stride=2), :] = f0
    dst[1, pl.ds(0, 96, stride=2), :] = jnp.where(low, f1, zero)
    dst[0, pl.ds(1, 96, stride=2), :] = pltpu.roll(jnp.where(low, f2, f1), 64, 1)
    dst[1, pl.ds(1, 96, stride=2), :] = jnp.where(low, pltpu.roll(f2, 64, 1), zero)


def load(ref, rows=B):
    return jnp.concatenate([ref[0, 0:rows, :], ref[1, 0:rows, :]], axis=1)


def store(ref, value):
    ref[0, 0:B, :] = value[:, :128]
    ref[1, 0:B, :] = value[:, 128:]


def flatten(even, odd):
    e0, e1 = even[:, :128], even[:, 128:]
    o0, o1 = odd[:, :128], odd[:, 128:]
    low = lanes_below(64, e0.shape)
    return e0, jnp.where(low, e1, pltpu.roll(o0, 64, 1)), pltpu.roll(jnp.where(low, o1, o0), 64, 1)


def split3(u):
    h = u.astype(BF16)
    rest = u - h.astype(F32)
    m = rest.astype(BF16)
    return h, m, (rest - m.astype(F32)).astype(BF16)


def split2(u):
    h = u.astype(BF16)
    return h, (u - h.astype(F32)).astype(BF16)


def factor_block(sa, r0):
    lo = 128 * (r0 // 128)
    hi = 384 if r0 + BLK <= 128 else 512
    width = hi - lo
    tiles = width // 128
    rows = sa[r0:r0 + BLK, lo:hi]
    diag = jnp.ones((BLK, 128), F32)
    ids = lax.broadcasted_iota(jnp.int32, (BLK, 128), 0)
    for sub in range(BLK // SUB):
        top = sub * SUB
        height = BLK - top
        live = rows[top:, :]
        col0 = r0 + top - lo
        cols = [jnp.broadcast_to(live[:, col0 + i:col0 + i + 1], (height, 128)) for i in range(SUB)]
        sub_ids = lax.broadcasted_iota(jnp.int32, (height, 128), 0)
        for j in range(SUB):
            cj = cols[j]
            pivot = cj[j:j + 1, :]
            f = jnp.where(sub_ids > j, cj * (1.0 / pivot), 0.0)
            diag = jnp.where(ids == top + j, pivot, diag)
            for i in range(j + 1, SUB):
                cols[i] = cols[i] - f * cj[i:i + 1, :]
            wide = jnp.concatenate([f] * tiles, axis=1)
            live = live - wide * live[j:j + 1, :]
        rows = live if top == 0 else jnp.concatenate([rows[:top], live], axis=0)
    u = rows * jnp.concatenate([lax.rsqrt(diag)] * tiles, axis=1)
    sa[r0:r0 + BLK, lo:hi] = u
    if r0 + BLK < B:
        h, m, l = split3(u)
        left = jnp.concatenate([h, h, m, h, m, l], axis=0)[:, :256 - lo]
        right = jnp.concatenate([h, m, h, l, m, h], axis=0)
        change = lax.dot_general(left, right, (((0,), (0,)), ((), ())), preferred_element_type=F32)
        sa[r0 + BLK:B, lo:hi] = sa[r0 + BLK:B, lo:hi] - change[r0 + BLK - lo:B - lo]


def start_tile(sa):
    r = lax.broadcasted_iota(jnp.int32, (B, 256), 0)
    c = lax.broadcasted_iota(jnp.int32, (B, 256), 1)
    sa[:, 256:512] = jnp.where(r == c, 1.0, 0.0).astype(F32)


def finish_tile(sa, linv, lfac):
    r = lax.broadcasted_iota(jnp.int32, (B, 256), 0)
    c = lax.broadcasted_iota(jnp.int32, (B, 256), 1)
    linv[0:B, :] = sa[:, 256:512]
    linv[B:256, :] = jnp.zeros((256 - B, 256), F32)
    u = jnp.where(r <= c, sa[:, 0:256], 0.0)
    full = jnp.concatenate([u, jnp.zeros((64, 256), F32)], axis=0)
    lfac[...] = full.T[0:B, :]


def nt(a, b):
    return lax.dot_general(a, b, (((1,), (1,)), ((), ())), precision=HIGH, preferred_element_type=F32)


def nn(a, b):
    return jnp.dot(a, b, precision=HIGH, preferred_element_type=F32)


def panel_step(t, g, linv):
    for p in range(t, 2):
        store(g.at[t, p], nt(load(g.at[t, p]), linv[t]))
    for s in range(t + 1, 3):
        for p in range(s - 1, 2):
            store(g.at[s, p], load(g.at[s, p]) - nt(load(g.at[t, p]), load(g.at[t, s - 1], 256)))


def own_step(t, g, linv, live):
    v = jnp.where(live[t], nt(load(g.at[t, 2]), linv[t]), 0.0)
    store(g.at[t, 2], v)
    for s in range(t + 1, 3):
        store(g.at[s, 2], load(g.at[s, 2]) - nt(v, load(g.at[t, s - 1], 256)))


def weights(g, linv, w, whi, wlo):
    def full(t, p):
        return load(g.at[t, p], 256)

    w2 = nn(load(g.at[2, 2]), linv[2])
    w1 = nn(load(g.at[1, 2]) - nn(w2, full(1, 1)), linv[1])
    w0 = nn(load(g.at[0, 2]) - nn(w2, full(0, 1)) - nn(w1, full(0, 0)), linv[0])
    for t, v in enumerate((w0, w1, w2)):
        store(w.at[t], v)
    for half in range(2):
        v = jnp.concatenate([w[i // 2, i % 2, pl.ds(half, 96, stride=2), :] for i in range(6)], axis=1)
        whi[96 * half:96 * half + 96, :], wlo[96 * half:96 * half + 96, :] = split2(v)


def special_tile(special, flat, g, lfac, which, same):
    x = jnp.where(which == 0, load(g.at[0, 2]), jnp.where(which == 1, load(g.at[1, 2]), load(g.at[2, 2])))
    f = jnp.where(which == 0, lfac[0], jnp.where(which == 1, lfac[1], lfac[2]))
    store(special, jnp.where(same, f, x))
    even = jnp.concatenate([special[i, pl.ds(0, 96, stride=2), :] for i in range(2)], axis=1)
    odd = jnp.concatenate([special[i, pl.ds(1, 96, stride=2), :] for i in range(2)], axis=1)
    for i, v in enumerate(flatten(even, odd)):
        flat[pl.ds(i, 96, stride=3), :] = v


def convert(rows, bt, bhi, blo):
    for t in range(3):
        unflatten(rows(t), bt.at[t])
    bhi[...], blo[...] = split2(jnp.concatenate([bt[i // 2, i % 2] for i in range(6)], axis=1))


def update(c, matrix, out, bhi, blo, whi, wlo, flat, j, panel, which, take):
    dims = (((1,), (1,)), ((), ()))
    both = lax.dot_general(jnp.concatenate([whi[...], wlo[...]], axis=0), bhi[...], dims, preferred_element_type=F32)
    change = both[:B] + both[B:] + lax.dot_general(whi[...], blo[...], dims, preferred_element_type=F32)
    change = jnp.concatenate([change, jnp.zeros((B, 64), F32)], axis=1)
    change = jnp.where(j > panel, change, 0.0)
    use = jnp.logical_and(take, j == panel + which)
    for i, v in enumerate(flatten(change[0:96], change[96:192])):
        old = matrix[c, pl.ds(i, 96, stride=3), :]
        out[c, pl.ds(i, 96, stride=3), :] = jnp.where(use, flat[pl.ds(i, 96, stride=3), :], old - v)


MESH = pl.DeviceIdType.MESH
N_SEM = 256
ORDER = [(0, 0), (1, 0), (1, 1), (2, 0), (2, 1), (2, 2)]
GROUPS = [(0, 1), (1, 2), (3, 3)]
LONG, SHORT = (48, 48, 48), (24, 24, 24)
LONG_AT, SHORT_AT = (0, 48, 96), (0, 24, 48)


def kernel(
    panel_ref, matrix, out,
    cut, got, pick, gotz0, gotz1, gotz2, tile0, tile1, tile2, rel, own, app, fresh, main, side,
    sa, linv, lfac, g, w, whi, wlo, bt, bhi, blo, special, flat,
    send_sem, recv_sem, quarter_sem, fresh_sem,
):
    panel = panel_ref[0]
    my_row, my_col = lax.axis_index("row"), lax.axis_index("col")
    x, core = lax.div(my_row, 16), lax.rem(my_row, 2)
    z = lax.rem(lax.div(my_row, 2), 8)
    xs = [x] + [lax.rem(x + d, 4) for d in range(1, 4)]
    ys = [my_col] + [lax.rem(my_col + d, 4) for d in range(1, 4)]
    zs = [z] + [lax.rem(z + d, 8) for d in range(1, 8)]
    cs = [core, 1 - core]
    x_rows, z_rows = [16 * v for v in xs], [2 * v for v in zs]
    known = {}
    here = lax.rem(my_row, 4)
    which = lax.rem(my_col - panel + 64, 4)
    gathered = [tile0, tile1, tile2]
    gotz = [gotz0, gotz1, gotz2]

    def at(dx, dc, dy, dz=0):
        key = (dx, dc, dy, dz % 8)
        if key not in known:
            known[key] = {"row": x_rows[dx] + z_rows[dz % 8] + cs[dc], "col": ys[dy]}
        return known[key]

    def at_quarter(u):
        return {"row": my_row - here + u, "col": here}

    group = [(dx, dc, dy) for dc in range(2) for dx in range(4) for dy in range(4)][1:]
    count = [0]
    sent = []

    def copy(src, dst, device):
        i = count[0]
        count[0] += 1
        c = pltpu.make_async_remote_copy(
            src_ref=src, dst_ref=dst, send_sem=send_sem.at[i], recv_sem=recv_sem.at[i],
            device_id=device, device_id_type=MESH,
        )
        c.start()
        sent.append(c)
        return c

    def arrive(copies):
        for c in copies:
            c.wait_recv()

    barrier = pltpu.get_barrier_semaphore()
    near = [at(*d) for d in group] + [at(0, 0, 0, dz) for dz in range(1, 8)]
    z_half = lax.rem(z, 2)
    across = z + 1 - 2 * z_half
    for dc in range(2):
        for dy in range(4):
            if dc or dy:
                near.append({"row": x_rows[0] + 2 * across + cs[dc], "col": ys[dy]})
    for device in near:
        pl.semaphore_signal(barrier, inc=1, device_id=device, device_id_type=MESH)

    g[...] = jnp.zeros_like(g)
    slot = jnp.minimum((panel + which) // 4, 15)
    mine = matrix[slot]
    rel[0] = mine
    for i in range(32):
        cut[i // 16, (i // 4) % 4, i % 4] = mine[9 * i:9 * i + 9]
    got[x, core, my_col] = cut[core, x, my_col]
    pl.semaphore_wait(barrier, len(near))

    pieces = []
    for dx, dc, dy in group:
        pieces.append(copy(
            cut.at[cs[dc], xs[dx], ys[dy]], got.at[x, core, my_col], at(dx, dc, dy),
        ))
    state = {}
    to_me = here == my_col
    quarters = []

    def send_quarters():
        for d in range(4):
            u = lax.rem(here + d, 4)
            part = rel.at[0, pl.ds(pl.multiple_of(72 * u, 8), 72)]
            quarters.append(pltpu.make_async_remote_copy(
                src_ref=part, dst_ref=fresh.at[my_col], send_sem=quarter_sem.at[d], recv_sem=fresh_sem.at[my_col],
                device_id=at_quarter(u), device_id_type=MESH,
            ))
        for c in quarters[1:]:
            c.start()

        @pl.when(jnp.logical_not(to_me))
        def _():
            quarters[0].start()

        @pl.when(to_me)
        def _():
            fresh[my_col] = rel[0, pl.ds(pl.multiple_of(72 * here, 8), 72), :]

    def quarters_ready():
        for q in range(4):
            c = pltpu.make_async_remote_copy(
                src_ref=rel.at[0, pl.ds(0, 72)], dst_ref=fresh.at[q], send_sem=quarter_sem.at[0], recv_sem=fresh_sem.at[q],
                device_id=at_quarter(0), device_id_type=MESH,
            )

            @pl.when(jnp.logical_not(jnp.logical_and(to_me, my_col == q)))
            def _():
                c.wait_recv()

    def quarters_sent():
        for c in quarters[1:]:
            c.wait_send()

        @pl.when(jnp.logical_not(to_me))
        def _():
            quarters[0].wait_send()

    def pick_rows():
        arrive(pieces)
        for n, (s, t) in enumerate(ORDER):
            r = panel + s
            pick[n] = got[r // 16, r % 2, (panel + t) % 4]
        state["z"] = []
        for (a, n), dst in zip(GROUPS, gotz):
            dst[z] = pick[a:a + n]
            state["z"].append([copy(pick.at[pl.ds(a, n)], dst.at[z], at(0, 0, 0, dz)) for dz in range(1, 8)])

    def gather(i):
        arrive(state["z"][i])
        a, n = GROUPS[i]
        tile = gathered[i]
        for m in range(n):
            r = panel + ORDER[a + m][0]
            tile[core, x, my_col, m] = gotz[i][(r // 2) % 8, m]
        mine = tile.at[core, x, my_col]
        members = group if i == 0 else [d for d in group if d[1] == 0]
        state[i] = [copy(mine, mine, at(*d)) for d in members]

    def other_core(i):
        arrive(state[i])
        half = gathered[i].at[core]
        state[i] = [copy(half, half, at(0, 1, 0))]

    def placed(i):
        arrive(state[i])
        a, n = GROUPS[i]
        for m in range(n):
            for p in range(32):
                app[a + m, 9 * p:9 * p + 9, :] = gathered[i][p // 16, (p // 4) % 4, p % 4, m]

    def row_start():
        state["y"] = [copy(rel.at[0], rel.at[d], at(0, 0, d)) for d in range(1, 4)]

    def row_ready():
        arrive(state["y"])
        for t in range(3):
            own[t] = rel[(my_col - panel - t + 64) % 4]
            unflatten(lambda o, t=t: own[t, pl.ds(o, 96, stride=3), :], g.at[t, 2])

    def main_block(d):
        return main.at[x, zs[d % 8], core]

    def pass_x(d):
        state["ax"][d] = [copy(main_block(d), main_block(d), at(k, 0, 0)) for k in range(1, 4)]

    def bulk_start():
        for t in range(3):
            v = fresh[(panel + t) % 4]
            main[x, z, core, LONG_AT[t]:LONG_AT[t] + LONG[t], :] = v[:LONG[t]]
            side[x, z, core, SHORT_AT[t]:SHORT_AT[t] + SHORT[t], :] = v[LONG[t]:]
        state["core"], state["ax"] = {}, {}
        main_ring(0)
        b = side.at[x, z, core]
        state["b"] = {}
        state["bx"] = {d: copy(b, b, at(d, 0, 0)) for d in range(1, 4)}
        side_ring(0, 0)

    def main_ring(step):
        def part(d, h):
            return main.at[x, zs[d % 8], core, pl.ds(72 * h, 72)]

        if step > 0:
            arrive(state["a"])
        if step < 3:
            state["a"] = [
                copy(main_block(-step), main_block(-step), at(0, 0, 0, 1)),
                copy(main_block(step), main_block(step), at(0, 0, 0, -1)),
            ]
        elif step == 3:
            state["a"] = [
                copy(part(-3, 0), part(-3, 0), at(0, 0, 0, 1)), copy(part(3, 1), part(3, 1), at(0, 0, 0, -1)),
            ]
        for d in ([0] if step == 0 else [-step, step] if step < 4 else [4]):
            pass_x(d)

    def main_core(*ds):
        for d in ds:
            arrive(state["ax"][d])
            a = main.at[:, zs[d % 8], core]
            state["core"][d] = [copy(a, a, at(0, 1, 0))] + state["core"].get(d, [])

    def side_ring(step, *ks):
        def block(k, d):
            return side.at[xs[k], zs[d % 8], core]

        def half(k, d, h):
            return side.at[xs[k], zs[d % 8], core, pl.ds(40 * h, 40 - 8 * h)]

        for k in ks:
            if step > 0:
                arrive(state["b"][k])
            elif k > 0:
                arrive([state["bx"][4 - k]])
            if step < 3:
                state["b"][k] = [
                    copy(block(k, -step), block(k, -step), at(0, 0, 0, 1)),
                    copy(block(k, step), block(k, step), at(0, 0, 0, -1)),
                ]
            elif step == 3:
                state["b"][k] = [
                    copy(half(k, -3, 0), half(k, -3, 0), at(0, 0, 0, 1)),
                    copy(half(k, 3, 1), half(k, 3, 1), at(0, 0, 0, -1)),
                ]

    def side_core(*ds):
        for d in ds:
            a = side.at[:, zs[d % 8], core]
            state["core"][d] = [copy(a, a, at(0, 1, 0))] + state["core"].get(d, [])

    def core_ready(*ds):
        for d in ds:
            arrive(state["core"][d])

    def panel_rows(k, m, t):
        def rows(o):
            parts = []
            for u in range(4):
                place = (k, 2 * m + u // 2, u % 2)
                parts.append(main[(*place, pl.ds(LONG_AT[t] + o, LONG[t] // 3, stride=3), slice(None))])
                parts.append(side[(*place, pl.ds(SHORT_AT[t] + o, SHORT[t] // 3, stride=3), slice(None))])
            return jnp.concatenate(parts, axis=0)

        return rows

    def app_tile(n, place):
        unflatten(lambda o: app[n, pl.ds(o, 96, stride=3), :], place)

    live = [my_row > panel + t for t in range(3)]
    rest = (1, 2, 3)
    agenda = {
        (0, 0): [lambda: other_core(1), lambda: other_core(2), row_start],
        (0, 1): [lambda: side_ring(1, *rest), lambda: side_core(0, -1, 1)],
        (0, 3): [lambda: main_ring(3), lambda: side_ring(3, 0)],
        (1, 1): [lambda: side_ring(2, *rest), lambda: side_core(-2, 2)],
        (1, 2): [lambda: main_ring(4), lambda: side_ring(4, 0)],
        (1, 4): [lambda: main_core(0, -1, 1)],
        (2, 2): [lambda: side_ring(3, *rest), lambda: side_core(-3, 3)],
        (2, 4): [lambda: main_core(-2, 2)],
    }

    send_quarters()
    pick_rows()
    quarters_ready()
    bulk_start()
    for i in range(3):
        gather(i)
    main_ring(1)
    side_ring(1, 0)
    side_ring(0, *rest)
    main_ring(2)
    side_ring(2, 0)
    placed(0)
    app_tile(0, bt.at[0, 0])
    for t in range(3):
        sa[:, 0:256] = load(bt.at[0, 0]) if t == 0 else load(g.at[t, t - 1])
        start_tile(sa)
        for blk in range(6):
            factor_block(sa, BLK * blk)
            for phase in agenda.get((t, blk), []):
                phase()
        finish_tile(sa, linv.at[t], lfac.at[t])
        if t == 0:
            placed(1)
            placed(2)
            for n, place in enumerate([(0, 0), (1, 0), (0, 1), (1, 1), (2, 1)]):
                app_tile(n + 1, g.at[place])
        panel_step(t, g, linv)
        if t == 1:
            row_ready()
            own_step(0, g, linv, live)
        if t > 0:
            own_step(t, g, linv, live)
    weights(g, linv, w, whi, wlo)
    tile = panel + which
    special_tile(special, flat, g, lfac, which, my_row == tile)
    take = jnp.logical_and(which < 3, my_row >= tile)
    half_z = lax.div(z, 2)

    def columns(i):
        m = lax.rem(half_z + i, 4)
        for k in range(4):
            convert(lambda t, k=k: panel_rows(k, m, t), bt.at[k], bhi.at[k], blo.at[k])
        for k in range(4):
            c = 4 * k + m
            update(c, matrix, out, bhi.at[k], blo.at[k], whi, wlo, flat, 4 * c + my_col, panel, which, take)

    main_core(-3, 3)
    core_ready(0, -1, 1)
    columns(0)
    side_ring(4, *rest)
    side_core(4)
    main_core(4)
    core_ready(-2, 2, -3, 3)
    columns(1)
    columns(3)
    for c in sent:
        c.wait_send()
    quarters_sent()
    core_ready(4)
    columns(2)


def body(matrix, panel_index):
    flat = matrix.reshape(16, 288, 128)
    V = pltpu.VMEM
    scratch = [
        V((2, 4, 4, 9, 128), F32), V((4, 2, 4, 9, 128), F32), V((6, 9, 128), F32), V((8, 1, 9, 128), F32), V((8, 2, 9, 128), F32), V((8, 3, 9, 128), F32),
        V((2, 4, 4, 1, 9, 128), F32), V((2, 4, 4, 2, 9, 128), F32), V((2, 4, 4, 3, 9, 128), F32),
        V((4, 288, 128), F32), V((3, 288, 128), F32), V((6, 288, 128), F32), V((4, 72, 128), F32),
        V((4, 8, 2, sum(LONG), 128), F32), V((4, 8, 2, sum(SHORT), 128), F32),
        V((B, 512), F32), V((3, 256, 256), F32), V((3, B, 256), F32), V((3, 3, 2, 256, 128), F32),
        V((3, 2, B, 128), F32), V((B, 768), BF16), V((B, 768), BF16), V((4, 3, 2, B, 128), F32),
        V((4, B, 768), BF16), V((4, B, 768), BF16), V((2, B, 128), F32), V((288, 128), F32),
        pltpu.SemaphoreType.DMA((N_SEM,)), pltpu.SemaphoreType.DMA((N_SEM,)),
        pltpu.SemaphoreType.DMA((4,)), pltpu.SemaphoreType.DMA((4,)),
    ]
    out = pl.pallas_call(
        kernel,
        out_shape=jax.ShapeDtypeStruct((16, 288, 128), F32),
        in_specs=[pl.BlockSpec(memory_space=pltpu.SMEM), pl.BlockSpec(memory_space=pltpu.VMEM)],
        out_specs=pl.BlockSpec(memory_space=pltpu.VMEM),
        scratch_shapes=scratch,
        compiler_params=pltpu.CompilerParams(collective_id=0, has_side_effects=True, vmem_limit_bytes=48 << 20),
        name="panel_steps",
    )(panel_index, flat)
    return out.reshape(matrix.shape)


def solution(mesh):
    in_specs = (P(None, "row", None, "col", None), P())
    out_specs = P(None, "row", None, "col", None)
    return jax.shard_map(body, mesh=mesh, in_specs=in_specs, out_specs=out_specs, check_vma=False)
```

```python
import jax
import jax.numpy as jnp
from jax import lax
from jax.experimental import pallas as pl
from jax.experimental.pallas import tpu as pltpu
from jax.sharding import PartitionSpec as P

B = 192
BLK = 32
SUB = 16
HIGH = lax.Precision.HIGHEST
F32 = jnp.float32
BF16 = jnp.bfloat16


def lanes_below(n, shape):
    return lax.broadcasted_iota(jnp.int32, shape, 1) < n


def unflatten(get, dst):
    f0, f1, f2 = get(0), get(1), get(2)
    low = lanes_below(64, f0.shape)
    zero = jnp.zeros_like(f0)
    dst[0, pl.ds(0, 96, stride=2), :] = f0
    dst[1, pl.ds(0, 96, stride=2), :] = jnp.where(low, f1, zero)
    dst[0, pl.ds(1, 96, stride=2), :] = pltpu.roll(jnp.where(low, f2, f1), 64, 1)
    dst[1, pl.ds(1, 96, stride=2), :] = jnp.where(low, pltpu.roll(f2, 64, 1), zero)


def load(ref, rows=B):
    return jnp.concatenate([ref[0, 0:rows, :], ref[1, 0:rows, :]], axis=1)


def store(ref, value):
    ref[0, 0:B, :] = value[:, :128]
    ref[1, 0:B, :] = value[:, 128:]


def flatten(even, odd):
    e0, e1 = even[:, :128], even[:, 128:]
    o0, o1 = odd[:, :128], odd[:, 128:]
    low = lanes_below(64, e0.shape)
    return e0, jnp.where(low, e1, pltpu.roll(o0, 64, 1)), pltpu.roll(jnp.where(low, o1, o0), 64, 1)


def split3(u):
    h = u.astype(BF16)
    rest = u - h.astype(F32)
    m = rest.astype(BF16)
    return h, m, (rest - m.astype(F32)).astype(BF16)


def split2(u):
    h = u.astype(BF16)
    return h, (u - h.astype(F32)).astype(BF16)


def factor_block(sa, r0):
    lo = 128 * (r0 // 128)
    hi = 384 if r0 + BLK <= 128 else 512
    width = hi - lo
    tiles = width // 128
    rows = sa[r0:r0 + BLK, lo:hi]
    diag = jnp.ones((BLK, 128), F32)
    ids = lax.broadcasted_iota(jnp.int32, (BLK, 128), 0)
    for sub in range(BLK // SUB):
        top = sub * SUB
        height = BLK - top
        live = rows[top:, :]
        col0 = r0 + top - lo
        cols = [jnp.broadcast_to(live[:, col0 + i:col0 + i + 1], (height, 128)) for i in range(SUB)]
        sub_ids = lax.broadcasted_iota(jnp.int32, (height, 128), 0)
        for j in range(SUB):
            cj = cols[j]
            pivot = cj[j:j + 1, :]
            f = jnp.where(sub_ids > j, cj * (1.0 / pivot), 0.0)
            diag = jnp.where(ids == top + j, pivot, diag)
            for i in range(j + 1, SUB):
                cols[i] = cols[i] - f * cj[i:i + 1, :]
            wide = jnp.concatenate([f] * tiles, axis=1)
            live = live - wide * live[j:j + 1, :]
        rows = live if top == 0 else jnp.concatenate([rows[:top], live], axis=0)
    u = rows * jnp.concatenate([lax.rsqrt(diag)] * tiles, axis=1)
    sa[r0:r0 + BLK, lo:hi] = u
    if r0 + BLK < B:
        h, m, l = split3(u)
        left = jnp.concatenate([h, h, m, h, m, l], axis=0)[:, :256 - lo]
        right = jnp.concatenate([h, m, h, l, m, h], axis=0)
        change = lax.dot_general(left, right, (((0,), (0,)), ((), ())), preferred_element_type=F32)
        sa[r0 + BLK:B, lo:hi] = sa[r0 + BLK:B, lo:hi] - change[r0 + BLK - lo:B - lo]


def start_tile(sa):
    r = lax.broadcasted_iota(jnp.int32, (B, 256), 0)
    c = lax.broadcasted_iota(jnp.int32, (B, 256), 1)
    sa[:, 256:512] = jnp.where(r == c, 1.0, 0.0).astype(F32)


def finish_tile(sa, linv, lfac):
    r = lax.broadcasted_iota(jnp.int32, (B, 256), 0)
    c = lax.broadcasted_iota(jnp.int32, (B, 256), 1)
    linv[0:B, :] = sa[:, 256:512]
    linv[B:256, :] = jnp.zeros((256 - B, 256), F32)
    u = jnp.where(r <= c, sa[:, 0:256], 0.0)
    full = jnp.concatenate([u, jnp.zeros((64, 256), F32)], axis=0)
    lfac[...] = full.T[0:B, :]


def nt(a, b):
    return lax.dot_general(a, b, (((1,), (1,)), ((), ())), precision=HIGH, preferred_element_type=F32)


def nn(a, b):
    return jnp.dot(a, b, precision=HIGH, preferred_element_type=F32)


def panel_step(t, g, linv):
    for p in range(t, 2):
        store(g.at[t, p], nt(load(g.at[t, p]), linv[t]))
    for s in range(t + 1, 3):
        for p in range(s - 1, 2):
            store(g.at[s, p], load(g.at[s, p]) - nt(load(g.at[t, p]), load(g.at[t, s - 1], 256)))


def own_step(t, g, linv, live):
    v = jnp.where(live[t], nt(load(g.at[t, 2]), linv[t]), 0.0)
    store(g.at[t, 2], v)
    for s in range(t + 1, 3):
        store(g.at[s, 2], load(g.at[s, 2]) - nt(v, load(g.at[t, s - 1], 256)))


def weights(g, linv, w, whi, wlo):
    def full(t, p):
        return load(g.at[t, p], 256)

    w2 = nn(load(g.at[2, 2]), linv[2])
    w1 = nn(load(g.at[1, 2]) - nn(w2, full(1, 1)), linv[1])
    w0 = nn(load(g.at[0, 2]) - nn(w2, full(0, 1)) - nn(w1, full(0, 0)), linv[0])
    for t, v in enumerate((w0, w1, w2)):
        store(w.at[t], v)
    for half in range(2):
        v = jnp.concatenate([w[i // 2, i % 2, pl.ds(half, 96, stride=2), :] for i in range(6)], axis=1)
        whi[96 * half:96 * half + 96, :], wlo[96 * half:96 * half + 96, :] = split2(v)


def special_tile(special, flat, g, lfac, which, same):
    x = jnp.where(which == 0, load(g.at[0, 2]), jnp.where(which == 1, load(g.at[1, 2]), load(g.at[2, 2])))
    f = jnp.where(which == 0, lfac[0], jnp.where(which == 1, lfac[1], lfac[2]))
    store(special, jnp.where(same, f, x))
    even = jnp.concatenate([special[i, pl.ds(0, 96, stride=2), :] for i in range(2)], axis=1)
    odd = jnp.concatenate([special[i, pl.ds(1, 96, stride=2), :] for i in range(2)], axis=1)
    for i, v in enumerate(flatten(even, odd)):
        flat[pl.ds(i, 96, stride=3), :] = v


def convert(rows, bt, bhi, blo):
    for t in range(3):
        unflatten(rows(t), bt.at[t])
    bhi[...], blo[...] = split2(jnp.concatenate([bt[i // 2, i % 2] for i in range(6)], axis=1))


def update(c, matrix, out, bhi, blo, whi, wlo, flat, j, panel, which, take):
    dims = (((1,), (1,)), ((), ()))
    both = lax.dot_general(jnp.concatenate([whi[...], wlo[...]], axis=0), bhi[...], dims, preferred_element_type=F32)
    change = both[:B] + both[B:] + lax.dot_general(whi[...], blo[...], dims, preferred_element_type=F32)
    change = jnp.concatenate([change, jnp.zeros((B, 64), F32)], axis=1)
    change = jnp.where(j > panel, change, 0.0)
    use = jnp.logical_and(take, j == panel + which)
    for i, v in enumerate(flatten(change[0:96], change[96:192])):
        old = matrix[c, pl.ds(i, 96, stride=3), :]
        out[c, pl.ds(i, 96, stride=3), :] = jnp.where(use, flat[pl.ds(i, 96, stride=3), :], old - v)


MESH = pl.DeviceIdType.MESH
N_SEM = 256
ORDER = [(0, 0), (1, 0), (1, 1), (2, 0), (2, 1), (2, 2)]
GROUPS = [(0, 1), (1, 2), (3, 3)]
LONG, SHORT = (48, 48, 48), (24, 24, 24)
LONG_AT, SHORT_AT = (0, 48, 96), (0, 24, 48)


def kernel(
    panel_ref, matrix, out,
    cut, got, pick, gotz0, gotz1, gotz2, tile0, tile1, tile2, rel, own, app, fresh, main, side,
    sa, linv, lfac, g, w, whi, wlo, bt, bhi, blo, special, flat,
    send_sem, recv_sem, quarter_sem, fresh_sem,
):
    panel = panel_ref[0]
    my_row, my_col = lax.axis_index("row"), lax.axis_index("col")
    x, core = lax.div(my_row, 16), lax.rem(my_row, 2)
    z = lax.rem(lax.div(my_row, 2), 8)
    xs = [x] + [lax.rem(x + d, 4) for d in range(1, 4)]
    ys = [my_col] + [lax.rem(my_col + d, 4) for d in range(1, 4)]
    zs = [z] + [lax.rem(z + d, 8) for d in range(1, 8)]
    cs = [core, 1 - core]
    x_rows, z_rows = [16 * v for v in xs], [2 * v for v in zs]
    known = {}
    here = lax.rem(my_row, 4)
    which = lax.rem(my_col - panel + 64, 4)
    gathered = [tile0, tile1, tile2]
    gotz = [gotz0, gotz1, gotz2]

    def at(dx, dc, dy, dz=0):
        key = (dx, dc, dy, dz % 8)
        if key not in known:
            known[key] = {"row": x_rows[dx] + z_rows[dz % 8] + cs[dc], "col": ys[dy]}
        return known[key]

    def at_quarter(u):
        return {"row": my_row - here + u, "col": here}

    group = [(dx, dc, dy) for dc in range(2) for dx in range(4) for dy in range(4)][1:]
    count = [0]
    sent = []

    def copy(src, dst, device):
        i = count[0]
        count[0] += 1
        c = pltpu.make_async_remote_copy(
            src_ref=src, dst_ref=dst, send_sem=send_sem.at[i], recv_sem=recv_sem.at[i],
            device_id=device, device_id_type=MESH,
        )
        c.start()
        sent.append(c)
        return c

    def arrive(copies):
        for c in copies:
            c.wait_recv()

    barrier = pltpu.get_barrier_semaphore()
    near = [at(*d) for d in group] + [at(0, 0, 0, dz) for dz in range(1, 8)]
    z_half = lax.rem(z, 2)
    across = z + 1 - 2 * z_half
    for dc in range(2):
        for dy in range(4):
            if dc or dy:
                near.append({"row": x_rows[0] + 2 * across + cs[dc], "col": ys[dy]})
    for device in near:
        pl.semaphore_signal(barrier, inc=1, device_id=device, device_id_type=MESH)

    g[...] = jnp.zeros_like(g)
    slot = jnp.minimum((panel + which) // 4, 15)
    mine = matrix[slot]
    rel[0] = mine
    for i in range(32):
        cut[i // 16, (i // 4) % 4, i % 4] = mine[9 * i:9 * i + 9]
    got[x, core, my_col] = cut[core, x, my_col]
    pl.semaphore_wait(barrier, len(near))

    pieces = []
    for dx, dc, dy in group:
        pieces.append(copy(
            cut.at[cs[dc], xs[dx], ys[dy]], got.at[x, core, my_col], at(dx, dc, dy),
        ))
    state = {}
    to_me = here == my_col
    quarters = []

    def send_quarters():
        for d in range(4):
            u = lax.rem(here + d, 4)
            part = rel.at[0, pl.ds(pl.multiple_of(72 * u, 8), 72)]
            quarters.append(pltpu.make_async_remote_copy(
                src_ref=part, dst_ref=fresh.at[my_col], send_sem=quarter_sem.at[d], recv_sem=fresh_sem.at[my_col],
                device_id=at_quarter(u), device_id_type=MESH,
            ))
        for c in quarters[1:]:
            c.start()

        @pl.when(jnp.logical_not(to_me))
        def _():
            quarters[0].start()

        @pl.when(to_me)
        def _():
            fresh[my_col] = rel[0, pl.ds(pl.multiple_of(72 * here, 8), 72), :]

    def quarters_ready():
        for q in range(4):
            c = pltpu.make_async_remote_copy(
                src_ref=rel.at[0, pl.ds(0, 72)], dst_ref=fresh.at[q], send_sem=quarter_sem.at[0], recv_sem=fresh_sem.at[q],
                device_id=at_quarter(0), device_id_type=MESH,
            )

            @pl.when(jnp.logical_not(jnp.logical_and(to_me, my_col == q)))
            def _():
                c.wait_recv()

    def quarters_sent():
        for c in quarters[1:]:
            c.wait_send()

        @pl.when(jnp.logical_not(to_me))
        def _():
            quarters[0].wait_send()

    def pick_rows():
        arrive(pieces)
        for n, (s, t) in enumerate(ORDER):
            r = panel + s
            pick[n] = got[r // 16, r % 2, (panel + t) % 4]
        state["z"] = []
        for (a, n), dst in zip(GROUPS, gotz):
            dst[z] = pick[a:a + n]
            state["z"].append([copy(pick.at[pl.ds(a, n)], dst.at[z], at(0, 0, 0, dz)) for dz in range(1, 8)])

    def gather(i):
        arrive(state["z"][i])
        a, n = GROUPS[i]
        tile = gathered[i]
        for m in range(n):
            r = panel + ORDER[a + m][0]
            tile[core, x, my_col, m] = gotz[i][(r // 2) % 8, m]
        mine = tile.at[core, x, my_col]
        members = group if i == 0 else [d for d in group if d[1] == 0]
        state[i] = [copy(mine, mine, at(*d)) for d in members]

    def other_core(i):
        arrive(state[i])
        half = gathered[i].at[core]
        state[i] = [copy(half, half, at(0, 1, 0))]

    def placed(i):
        arrive(state[i])
        a, n = GROUPS[i]
        for m in range(n):
            for p in range(32):
                app[a + m, 9 * p:9 * p + 9, :] = gathered[i][p // 16, (p // 4) % 4, p % 4, m]

    def row_start():
        state["y"] = [copy(rel.at[0], rel.at[d], at(0, 0, d)) for d in range(1, 4)]

    def row_ready():
        arrive(state["y"])
        for t in range(3):
            own[t] = rel[(my_col - panel - t + 64) % 4]
            unflatten(lambda o, t=t: own[t, pl.ds(o, 96, stride=3), :], g.at[t, 2])

    def main_block(d):
        return main.at[x, zs[d % 8], core]

    def pass_x(d):
        state["ax"][d] = [copy(main_block(d), main_block(d), at(k, 0, 0)) for k in range(1, 4)]

    def bulk_start():
        for t in range(3):
            v = fresh[(panel + t) % 4]
            main[x, z, core, LONG_AT[t]:LONG_AT[t] + LONG[t], :] = v[:LONG[t]]
            side[x, z, core, SHORT_AT[t]:SHORT_AT[t] + SHORT[t], :] = v[LONG[t]:]
        state["core"], state["ax"] = {}, {}
        main_ring(0)
        b = side.at[x, z, core]
        state["b"] = {}
        state["bx"] = {d: copy(b, b, at(d, 0, 0)) for d in range(1, 4)}
        side_ring(0, 0)

    def main_ring(step):
        def part(d, h):
            return main.at[x, zs[d % 8], core, pl.ds(72 * h, 72)]

        if step > 0:
            arrive(state["a"])
        if step < 3:
            state["a"] = [
                copy(main_block(-step), main_block(-step), at(0, 0, 0, 1)),
                copy(main_block(step), main_block(step), at(0, 0, 0, -1)),
            ]
        elif step == 3:
            state["a"] = [
                copy(part(-3, 0), part(-3, 0), at(0, 0, 0, 1)), copy(part(3, 1), part(3, 1), at(0, 0, 0, -1)),
            ]
        for d in ([0] if step == 0 else [-step, step] if step < 4 else [4]):
            pass_x(d)

    def main_core(*ds):
        for d in ds:
            arrive(state["ax"][d])
            a = main.at[:, zs[d % 8], core]
            state["core"][d] = [copy(a, a, at(0, 1, 0))] + state["core"].get(d, [])

    def side_ring(step, *ks):
        def block(k, d):
            return side.at[xs[k], zs[d % 8], core]

        def half(k, d, h):
            return side.at[xs[k], zs[d % 8], core, pl.ds(40 * h, 40 - 8 * h)]

        for k in ks:
            if step > 0:
                arrive(state["b"][k])
            elif k > 0:
                arrive([state["bx"][4 - k]])
            if step < 3:
                state["b"][k] = [
                    copy(block(k, -step), block(k, -step), at(0, 0, 0, 1)),
                    copy(block(k, step), block(k, step), at(0, 0, 0, -1)),
                ]
            elif step == 3:
                state["b"][k] = [
                    copy(half(k, -3, 0), half(k, -3, 0), at(0, 0, 0, 1)),
                    copy(half(k, 3, 1), half(k, 3, 1), at(0, 0, 0, -1)),
                ]

    def side_core(*ds):
        for d in ds:
            a = side.at[:, zs[d % 8], core]
            state["core"][d] = [copy(a, a, at(0, 1, 0))] + state["core"].get(d, [])

    def core_ready(*ds):
        for d in ds:
            arrive(state["core"][d])

    def panel_rows(k, m, t):
        def rows(o):
            parts = []
            for u in range(4):
                place = (k, 2 * m + u // 2, u % 2)
                parts.append(main[(*place, pl.ds(LONG_AT[t] + o, LONG[t] // 3, stride=3), slice(None))])
                parts.append(side[(*place, pl.ds(SHORT_AT[t] + o, SHORT[t] // 3, stride=3), slice(None))])
            return jnp.concatenate(parts, axis=0)

        return rows

    def app_tile(n, place):
        unflatten(lambda o: app[n, pl.ds(o, 96, stride=3), :], place)

    live = [my_row > panel + t for t in range(3)]
    rest = (1, 2, 3)
    agenda = {
        (0, 0): [lambda: other_core(1)],
        (0, 1): [lambda: other_core(2), row_start, lambda: main_ring(2), lambda: side_ring(2, 0)],
        (0, 3): [lambda: side_ring(1, *rest), lambda: side_core(0, -1, 1)],
        (0, 5): [lambda: main_ring(3), lambda: side_ring(3, 0)],
        (1, 1): [lambda: side_ring(2, *rest), lambda: side_core(-2, 2)],
        (1, 3): [lambda: main_ring(4), lambda: side_ring(4, 0)],
        (1, 5): [lambda: main_core(0, -1, 1)],
        (2, 2): [lambda: side_ring(3, *rest), lambda: side_core(-3, 3)],
        (2, 4): [lambda: main_core(-2, 2)],
    }

    send_quarters()
    pick_rows()
    quarters_ready()
    bulk_start()
    for i in range(3):
        gather(i)
    main_ring(1)
    side_ring(1, 0)
    side_ring(0, *rest)
    placed(0)
    app_tile(0, bt.at[0, 0])
    for t in range(3):
        sa[:, 0:256] = load(bt.at[0, 0]) if t == 0 else load(g.at[t, t - 1])
        start_tile(sa)
        for blk in range(6):
            factor_block(sa, BLK * blk)
            for phase in agenda.get((t, blk), []):
                phase()
        finish_tile(sa, linv.at[t], lfac.at[t])
        if t == 0:
            placed(1)
            placed(2)
            for n, place in enumerate([(0, 0), (1, 0), (0, 1), (1, 1), (2, 1)]):
                app_tile(n + 1, g.at[place])
        panel_step(t, g, linv)
        if t == 1:
            row_ready()
            own_step(0, g, linv, live)
        if t > 0:
            own_step(t, g, linv, live)
    weights(g, linv, w, whi, wlo)
    tile = panel + which
    special_tile(special, flat, g, lfac, which, my_row == tile)
    take = jnp.logical_and(which < 3, my_row >= tile)
    half_z = lax.div(z, 2)

    def columns(i):
        m = lax.rem(half_z + i, 4)
        for k in range(4):
            convert(lambda t, k=k: panel_rows(k, m, t), bt.at[k], bhi.at[k], blo.at[k])
        for k in range(4):
            c = 4 * k + m
            update(c, matrix, out, bhi.at[k], blo.at[k], whi, wlo, flat, 4 * c + my_col, panel, which, take)

    main_core(-3, 3)
    core_ready(0, -1, 1)
    columns(0)
    side_ring(4, *rest)
    side_core(4)
    main_core(4)
    core_ready(-2, 2, -3, 3)
    columns(1)
    columns(3)
    for c in sent:
        c.wait_send()
    quarters_sent()
    core_ready(4)
    columns(2)


def body(matrix, panel_index):
    flat = matrix.reshape(16, 288, 128)
    V = pltpu.VMEM
    scratch = [
        V((2, 4, 4, 9, 128), F32), V((4, 2, 4, 9, 128), F32), V((6, 9, 128), F32), V((8, 1, 9, 128), F32), V((8, 2, 9, 128), F32), V((8, 3, 9, 128), F32),
        V((2, 4, 4, 1, 9, 128), F32), V((2, 4, 4, 2, 9, 128), F32), V((2, 4, 4, 3, 9, 128), F32),
        V((4, 288, 128), F32), V((3, 288, 128), F32), V((6, 288, 128), F32), V((4, 72, 128), F32),
        V((4, 8, 2, sum(LONG), 128), F32), V((4, 8, 2, sum(SHORT), 128), F32),
        V((B, 512), F32), V((3, 256, 256), F32), V((3, B, 256), F32), V((3, 3, 2, 256, 128), F32),
        V((3, 2, B, 128), F32), V((B, 768), BF16), V((B, 768), BF16), V((4, 3, 2, B, 128), F32),
        V((4, B, 768), BF16), V((4, B, 768), BF16), V((2, B, 128), F32), V((288, 128), F32),
        pltpu.SemaphoreType.DMA((N_SEM,)), pltpu.SemaphoreType.DMA((N_SEM,)),
        pltpu.SemaphoreType.DMA((4,)), pltpu.SemaphoreType.DMA((4,)),
    ]
    out = pl.pallas_call(
        kernel,
        out_shape=jax.ShapeDtypeStruct((16, 288, 128), F32),
        in_specs=[pl.BlockSpec(memory_space=pltpu.SMEM), pl.BlockSpec(memory_space=pltpu.VMEM)],
        out_specs=pl.BlockSpec(memory_space=pltpu.VMEM),
        scratch_shapes=scratch,
        compiler_params=pltpu.CompilerParams(collective_id=0, has_side_effects=True, vmem_limit_bytes=48 << 20),
        name="panel_steps",
    )(panel_index, flat)
    return out.reshape(matrix.shape)


def solution(mesh):
    in_specs = (P(None, "row", None, "col", None), P())
    out_specs = P(None, "row", None, "col", None)
    return jax.shard_map(body, mesh=mesh, in_specs=in_specs, out_specs=out_specs, check_vma=False)
```
